128 devices in a mesh: enc: 8 (over z, y_hi), grp: 8 (over x, y_lo), seq: 2 (over core).
Axes of the slice: x: 4, y: 4 (y_hi: 2, y_lo: 2; y = y_hi * 2 + y_lo), z: 4, core: 2. Of those that a mesh axis runs over, the one named last changes fastest.
Arguments:
- features: bfloat16 [8, 8, 8, 160, 256], P('grp', None, 'seq', 'enc')
- conv_weight: bfloat16 [3, 3, 3, 256, 256], replicated, may hold values from -0.078125 to 0.078125
- latent_weight: bfloat16 [256, 16], replicated, may hold values from -0.375 to 0.375
- lengths: int32 [8], replicated, may hold values from 1 to 8, as said below
- clip_order: int32 [8], replicated, may hold values from 0 to 7, as said below
- embed_weight: bfloat16 [64, 3072], replicated, may hold values from -0.75 to 0.75
- qkv_weight: bfloat16 [3072, 3, 3072], P(None, None, ('enc', 'seq'))
Outputs:
- attended: bfloat16 [8, 8, 4, 80, 3072], P('grp', None, 'seq', 'enc')
The draws below stay inside these ranges and needn't reach their ends.
Inputs may be any that keep to these rules, and one draw needn't show every extreme that they name: `lengths`: some clip has exactly 8 frames. `clip_order`: every replica is named by exactly one clip.
All inputs are finite; a program needn't handle non-finite values.
Results may differ from the reference program's by a relative error of at most 0.022.
The reference program's roundings to bfloat16 on the way (of `activated`, `hidden`, `latent`, `patches`, `embedded`, `queries` and `weights`) count: a program that leaves them out, or rounds other values in their place, can miss the bound.
Values may be sent and summed in bfloat16 or wider, within the bound.
A program may use at most 128 MiB of HBM per device.

```python
import jax
import jax.numpy as jnp
from jax import lax

C = 256
LAT = 16
D = 3072
HEADS = 48
HD = 64
MAXF = 8
ROWS = 8
W = 160
CLIPS = 8
TOK_CLIP = 2560


def draw_features(key, part):
    key = jax.random.fold_in(key, 11)
    base_key = jax.random.fold_in(key, 0)
    base = jax.random.normal(base_key, (CLIPS, MAXF, ROWS, W, C), jnp.float32)
    base = jnp.clip(base, -6.0, 6.0)
    return base.astype(jnp.bfloat16)


def draw_lengths(key, part):
    key = jax.random.fold_in(key, 12)
    len_key, pick_key = jax.random.split(key)
    drawn = jax.random.randint(len_key, (CLIPS,), 1, MAXF + 1, jnp.int32)
    chosen = jax.random.randint(pick_key, (), 0, CLIPS, jnp.int32)
    return jnp.where(jnp.arange(CLIPS, dtype=jnp.int32) == chosen, MAXF, drawn).astype(jnp.int32)


def draw_clip_order(key, part):
    key = jax.random.fold_in(key, 977)
    scores = jax.random.randint(key, (CLIPS,), 0, 1 << 20, jnp.int32)
    scores = scores * CLIPS + jnp.arange(CLIPS, dtype=jnp.int32)
    return jnp.argsort(scores, stable=True).astype(jnp.int32)


def draw_qkv_weight(key, part):
    key = jax.random.fold_in(key, 13)
    query_key, key_key, value_key = jax.random.split(key, 3)
    spread = D ** (-0.5)
    query_part = jax.random.normal(query_key, (D, HEADS * HD), jnp.float32) * spread
    key_part = jax.random.normal(key_key, (D, HEADS * HD), jnp.float32) * spread
    value_part = jax.random.normal(value_key, (D, HEADS * HD), jnp.float32) * spread
    return jnp.stack([query_part, key_part, value_part], axis=1).astype(jnp.bfloat16)


def normal_values(rng, dims, scale, most, kind=jnp.bfloat16):
    array = scale * jax.random.normal(rng, dims, jnp.float32)
    return jnp.clip(array, min=-most, max=most).astype(kind)


def setup_inputs(seed: int = 0) -> dict:
    key_list = jax.random.split(jax.random.key(seed), 8)
    features = draw_features(jax.random.fold_in(key_list[7], 71), 0)
    conv_weight = normal_values(key_list[1], (3, 3, 3, C, C), (27 * C) ** -0.5, 0.078125)
    latent_weight = normal_values(key_list[2], (C, LAT), C ** -0.5, 0.375)
    lengths = draw_lengths(jax.random.fold_in(key_list[7], 71), 0)
    clip_order = draw_clip_order(jax.random.fold_in(key_list[7], 71), 0)
    embed_weight = normal_values(key_list[5], (4 * LAT, D), (4 * LAT) ** -0.5, 0.75)
    qkv_weight = draw_qkv_weight(jax.random.fold_in(key_list[7], 71), 0)
    return {"features": features, "conv_weight": conv_weight, "latent_weight": latent_weight, "lengths": lengths, "clip_order": clip_order, "embed_weight": embed_weight, "qkv_weight": qkv_weight}


def reference(features, conv_weight, latent_weight, lengths, clip_order, embed_weight, qkv_weight):
    flat_conv = conv_weight.reshape(27 * C, C)
    frame_ids = jnp.arange(MAXF, dtype=jnp.int32)

    def encode(operands):
        clip, length = operands
        activated = jax.nn.silu(clip.astype(jnp.float32)).astype(jnp.bfloat16)
        padded = jnp.pad(activated, ((2, 0), (1, 1), (1, 1), (0, 0)))
        columns = []
        for shift_t in range(3):
            for shift_y in range(3):
                for shift_x in range(3):
                    columns.append(padded[shift_t:shift_t + MAXF, shift_y:shift_y + ROWS, shift_x:shift_x + W, :])
        stacked = jnp.concatenate(columns, axis=-1).reshape(-1, 27 * C)
        pre = jnp.dot(stacked, flat_conv, preferred_element_type=jnp.float32)
        hidden = (clip.astype(jnp.float32).reshape(-1, C) + pre).astype(jnp.bfloat16)
        latent = jnp.dot(hidden, latent_weight, preferred_element_type=jnp.float32).reshape(MAXF, ROWS, W, LAT)
        latent = jnp.where((frame_ids < length)[:, None, None, None], latent, 0.0).astype(jnp.bfloat16)
        patches = latent.reshape(MAXF, ROWS // 2, 2, W // 2, 2, LAT).transpose(0, 1, 3, 2, 4, 5)
        return patches.reshape(MAXF * (ROWS // 2) * (W // 2), 4 * LAT)

    patches = lax.map(encode, (features, lengths))
    source = jnp.zeros((CLIPS,), jnp.int32).at[clip_order].set(jnp.arange(CLIPS, dtype=jnp.int32))
    per_frame = (ROWS // 2) * (W // 2)
    token_frame = jnp.arange(TOK_CLIP, dtype=jnp.int32) // per_frame
    scale = HD ** -0.5

    def train(replica):
        tokens = patches[source[replica]]
        clip_len = lengths[source[replica]]
        valid = token_frame < clip_len
        embedded = jnp.dot(tokens, embed_weight, preferred_element_type=jnp.float32).astype(jnp.bfloat16)
        queries = jnp.dot(embedded, qkv_weight[:, 0, :], preferred_element_type=jnp.float32).astype(jnp.bfloat16)
        keys_all = jnp.dot(embedded, qkv_weight[:, 1, :], preferred_element_type=jnp.float32).astype(jnp.bfloat16)
        values_all = jnp.dot(embedded, qkv_weight[:, 2, :], preferred_element_type=jnp.float32).astype(jnp.bfloat16)
        queries = queries.reshape(TOK_CLIP, HEADS, HD).transpose(1, 0, 2)
        keys_all = keys_all.reshape(TOK_CLIP, HEADS, HD).transpose(1, 0, 2)
        values_all = values_all.reshape(TOK_CLIP, HEADS, HD).transpose(1, 0, 2)

        def one_head(operands):
            head_q, head_k, head_v = operands
            scores = jnp.dot(head_q, head_k.T, preferred_element_type=jnp.float32) * scale
            scores = jnp.where(valid[None, :], scores, -1e30)
            peak = jnp.max(scores, axis=-1, keepdims=True)
            expo = jnp.exp(scores - peak)
            weights = (expo / jnp.sum(expo, axis=-1, keepdims=True)).astype(jnp.bfloat16)
            return jnp.dot(weights, head_v, preferred_element_type=jnp.float32)

        outputs = lax.map(one_head, (queries, keys_all, values_all))
        outputs = outputs.transpose(1, 0, 2).reshape(TOK_CLIP, HEADS * HD)
        outputs = jnp.where(valid[:, None], outputs, 0.0).astype(jnp.bfloat16)
        return outputs.reshape(MAXF, ROWS // 2, W // 2, HEADS * HD)

    return lax.map(train, jnp.arange(CLIPS, dtype=jnp.int32))
```

```python
import functools
import math

import jax
import jax.numpy as jnp
from jax import lax
from jax.experimental import pallas as pl
from jax.experimental.pallas import tpu as pltpu
from jax.sharding import PartitionSpec as P

HD = 64
LANES = 128
MESH = pl.DeviceIdType.MESH
F32 = jnp.float32
BF16 = jnp.bfloat16
NT = (((1,), (1,)), ((), ()))


def dot_nt(a, b):
    return lax.dot_general(a, b, NT, preferred_element_type=F32)


def lane_ids(rows):
    return lax.broadcasted_iota(jnp.int32, (rows, LANES), 1)


def silu(v):
    return (v / (1.0 + jnp.exp(-v))).astype(BF16)


def kernel(
    dims,
    feat,
    conv_hbm,
    lat_w,
    lengths,
    order,
    emb_hbm,
    qkv_hbm,
    out,
    conv_w,
    emb,
    qkv,
    row_out,
    col_out,
    row_in,
    col_in,
    corner_in,
    padded,
    even,
    odd,
    patch,
    pool,
    chosen,
    gathered,
    tokens,
    key_tokens,
    wide,
    wq,
    wk,
    wv,
    queries,
    keys_t,
    values,
    scores,
    probs,
    parcel,
    landed,
    load_sem,
    halo_send,
    halo_recv,
    pool_send,
    pool_recv,
    gather_send,
    gather_recv,
    parcel_send,
    parcel_recv,
):
    enc_n, grp_n, seq_n = dims
    dev_n = enc_n * seq_n
    enc, grp, seq = lax.axis_index("enc"), lax.axis_index("grp"), lax.axis_index("seq")
    me = enc * seq_n + seq
    other = 1 - seq
    rows_y, tile_w, frames, channels = feat.shape
    wide_x = tile_w + 2
    half = patch.shape[0]
    half_all = dev_n * half
    tok_all = 2 * half_all

    loads = []
    for slot, (src, dst) in enumerate(
        (
            (conv_hbm, conv_w),
            (qkv_hbm, qkv),
            (emb_hbm, emb.at[pl.ds(0, HD)]),
            (emb_hbm, emb.at[pl.ds(HD, HD)]),
        )
    ):
        copy = pltpu.make_async_copy(src, dst, load_sem.at[slot])
        copy.start()
        loads.append(copy)

    barrier = pltpu.get_barrier_semaphore()

    def greet_clip(step, carry):
        peer = lax.rem(me + step, dev_n)
        pl.semaphore_signal(
            barrier,
            inc=1,
            device_id={"enc": peer // seq_n, "seq": lax.rem(peer, seq_n)},
            device_id_type=MESH,
        )
        return carry

    def greet_pool(step, carry):
        pl.semaphore_signal(
            barrier,
            inc=1,
            device_id={"grp": lax.rem(grp + step, grp_n)},
            device_id_type=MESH,
        )
        return carry

    lax.fori_loop(1, dev_n, greet_clip, 0)
    lax.fori_loop(1, grp_n, greet_pool, 0)

    edge_y = jnp.where(seq == 0, rows_y - 1, 0)
    row_out[...] = silu(feat[edge_y].reshape(tile_w * frames, channels))
    for side, x in enumerate((0, tile_w - 1)):
        col_out[side] = silu(feat[:, x].reshape(rows_y * frames, channels))
    pl.semaphore_wait(barrier, dev_n - 1 + grp_n - 1)
    left, right = lax.rem(enc + enc_n - 1, enc_n), lax.rem(enc + 1, enc_n)
    corner = 2 * frames
    corner_from = pl.multiple_of(jnp.where(seq == 0, rows_y * frames - corner, 0), corner)
    halos = [
        pltpu.make_async_remote_copy(
            src_ref=row_out,
            dst_ref=row_in,
            send_sem=halo_send.at[0],
            recv_sem=halo_recv.at[0],
            device_id={"seq": other},
            device_id_type=MESH,
        )
    ]
    for side, target in enumerate((left, right)):
        halos.append(
            pltpu.make_async_remote_copy(
                src_ref=col_out.at[side],
                dst_ref=col_in.at[1 - side],
                send_sem=halo_send.at[1 + side],
                recv_sem=halo_recv.at[1 + side],
                device_id={"enc": target},
                device_id_type=MESH,
            )
        )
        halos.append(
            pltpu.make_async_remote_copy(
                src_ref=col_out.at[side, pl.ds(corner_from, corner)],
                dst_ref=corner_in.at[1 - side],
                send_sem=halo_send.at[3 + side],
                recv_sem=halo_recv.at[3 + side],
                device_id={"enc": target, "seq": other},
                device_id_type=MESH,
            )
        )
    for copy in halos:
        copy.start()

    line = wide_x * frames

    def place(y, x, value):
        start = (y * wide_x + x) * frames
        padded[pl.ds(start, value.shape[0])] = value

    for y in range(rows_y):
        inner = silu(feat[y].reshape(tile_w * frames, channels)).astype(F32)
        place(y + 1, 1, inner)

    for copy in loads[1:]:
        copy.wait()
    folded = dot_nt(qkv[...], emb[...])
    high = folded.astype(BF16).astype(F32)
    low = folded - high
    lane = lane_ids(folded.shape[0])
    for part in range(2):
        keep = (lane >= HD) if part else (lane < HD)
        wide[part, :, pl.ds(0, LANES)] = jnp.where(keep, high, 0.0).astype(BF16)
        wide[part, :, pl.ds(LANES, LANES)] = jnp.where(keep, low, 0.0).astype(BF16)
    heads = qkv.shape[0] // 3 // HD
    for part in range(2):
        for place_h in range(heads):
            source_h = lax.rem(place_h + seq, heads)
            for which, dst in enumerate((wq, wk, wv)):
                start = pl.multiple_of((which * heads + source_h) * HD, HD)
                block = wide[part, pl.ds(start, HD)]
                dst[part, place_h, pl.ds(0, HD)] = block
                dst[part, place_h, pl.ds(HD, HD)] = (
                    jnp.zeros_like(block) if which == 2 else block
                )

    for copy in halos:
        copy.wait()
    row = row_in[...].astype(F32)
    place(0, 1, jnp.where(seq == 1, row, 0.0))
    place(rows_y + 1, 1, jnp.where(seq == 0, row, 0.0))
    for side, x in enumerate((0, wide_x - 1)):
        present = (enc > 0) if side == 0 else (enc < enc_n - 1)
        column = jnp.where(present, col_in[side].astype(F32), 0.0)
        for y in range(rows_y):
            place(y + 1, x, column[y * frames : (y + 1) * frames])
        cells = jnp.where(present, corner_in[side].astype(F32), 0.0)
        place(0, x, jnp.where(seq == 1, cells[frames:], 0.0))
        place(rows_y + 1, x, jnp.where(seq == 0, cells[:frames], 0.0))

    frame = None
    for dst, offset in ((even, 0), (odd, frames)):
        rows = dst.shape[0]
        cells = padded[pl.ds(offset, rows)].reshape(rows // frames, frames, channels)
        frame = lax.broadcasted_iota(jnp.int32, cells.shape, 1)
        for shift in range(3):
            back = 2 - shift
            moved = cells if back == 0 else pltpu.roll(cells, back, 1)
            moved = jnp.where(frame >= back, moved, 0.0)
            dst[:, pl.ds(shift * channels, channels)] = moved.reshape(rows, channels).astype(BF16)

    loads[0].wait()
    span = ((rows_y - 1) * wide_x + tile_w) * frames
    pre = None
    for dy in range(3):
        for dx in range(3):
            src = odd if dx == 1 else even
            start = (dy * wide_x + (dx if dx == 2 else 0)) * frames
            for dt in range(3):
                term = jnp.dot(
                    src[pl.ds(start, span), pl.ds(dt * channels, channels)],
                    conv_w[(dt * 3 + dy) * 3 + dx],
                    preferred_element_type=F32,
                )
                pre = term if pre is None else pre + term

    lat_ch = lat_w.shape[0]
    own_len = lengths[grp]
    packed = None
    for y in range(rows_y):
        body = pre[y * line : y * line + tile_w * frames] + feat[y].reshape(
            tile_w * frames, channels
        )
        body = body.reshape(tile_w // 2, 2, frames, channels)
        for b in range(2):
            hidden = body[:, b].reshape(half, channels).astype(BF16)
            first = (y * 2 + b) * lat_ch
            parts = []
            if first:
                parts.append(jnp.zeros((first, channels), BF16))
            parts.append(lat_w[...])
            if first + lat_ch < LANES:
                parts.append(jnp.zeros((LANES - first - lat_ch, channels), BF16))
            term = dot_nt(hidden, jnp.concatenate(parts, axis=0))
            packed = term if packed is None else packed + term
    frame = lax.rem(lax.broadcasted_iota(jnp.int32, (half, LANES), 0), frames)
    patch[...] = jnp.where(frame < own_len, packed, 0.0).astype(BF16)

    source = jnp.int32(0)
    for n in range(grp_n):
        source = source + jnp.where(order[n] == grp, n, 0)
    source = jnp.minimum(source, grp_n - 1)
    clip_len = lengths[source]

    def pool_copy(peer, slot):
        return pltpu.make_async_remote_copy(
            src_ref=patch,
            dst_ref=pool.at[slot],
            send_sem=pool_send.at[peer],
            recv_sem=pool_recv.at[slot],
            device_id={"grp": peer},
            device_id_type=MESH,
        )

    def pool_start(step, carry):
        pool_copy(lax.rem(grp + step, grp_n), grp).start()
        return carry

    def pool_wait(step, carry):
        peer = lax.rem(grp + step, grp_n)
        pool_copy(peer, peer).wait()
        return carry

    lax.fori_loop(1, grp_n, pool_start, 0)
    pool[grp] = patch[...]
    lax.fori_loop(1, grp_n, pool_wait, 0)
    chosen[...] = pool[source]

    def gather_copy(peer, slot):
        return pltpu.make_async_remote_copy(
            src_ref=chosen,
            dst_ref=gathered.at[slot],
            send_sem=gather_send.at[peer],
            recv_sem=gather_recv.at[slot],
            device_id={"enc": peer // seq_n, "seq": lax.rem(peer, seq_n)},
            device_id_type=MESH,
        )

    def gather_start(step, carry):
        gather_copy(lax.rem(me + step, dev_n), me).start()
        return carry

    def gather_wait(step, carry):
        peer = lax.rem(me + step, dev_n)
        gather_copy(peer, peer).wait()
        return carry

    lax.fori_loop(1, dev_n, gather_start, 0)
    gathered[me] = chosen[...]
    lax.fori_loop(1, dev_n, gather_wait, 0)

    cells = gathered[...].reshape(half_all, LANES)
    tokens[:, pl.ds(0, LANES)] = cells
    tokens[:, pl.ds(LANES, LANES)] = cells
    wide_cells = cells.astype(F32).reshape(half_all // frames, frames, LANES)
    frame = lax.broadcasted_iota(jnp.int32, wide_cells.shape, 1)
    kept = jnp.where(frame < clip_len, wide_cells, wide_cells[:, :1])
    kept = kept.reshape(half_all, LANES).astype(BF16)
    key_tokens[:, pl.ds(0, LANES)] = kept
    key_tokens[:, pl.ds(LANES, LANES)] = kept

    factor = HD**-0.5 * math.log2(math.e)
    lane = lane_ids(half_all)
    frame = lax.rem(lax.broadcasted_iota(jnp.int32, (half_all, LANES), 0), frames)
    counted = jnp.where(frame < clip_len, 1.0, 0.0)
    for head in range(heads):
        for part in range(2):
            query = dot_nt(tokens[...], wq[part, head]).astype(BF16).astype(F32) * factor
            high = query.astype(BF16).astype(F32)
            pair = jnp.where(lane < HD, high, query - high).astype(BF16)
            queries[head, :, pl.ds(part * half, half)] = pair.reshape(dev_n, half, LANES)
            keys_t[head, :, pl.ds(part * half_all, half_all)] = dot_nt(
                wk[part, head], key_tokens[...]
            ).astype(BF16)
            value = dot_nt(tokens[...], wv[part, head])
            values[head, pl.ds(part * half_all, half_all)] = jnp.where(
                lane == HD, counted, value
            ).astype(BF16)

    chunk = 256
    tok = 2 * half
    lane = lane_ids(tok)
    frame = lax.rem(lax.broadcasted_iota(jnp.int32, (tok, LANES), 0), frames)
    alive = frame < clip_len

    def parcel_copy(peer, slot):
        return pltpu.make_async_remote_copy(
            src_ref=parcel.at[peer],
            dst_ref=landed.at[slot],
            send_sem=parcel_send.at[peer],
            recv_sem=parcel_recv.at[slot],
            device_id={"enc": peer // seq_n, "seq": lax.rem(peer, seq_n)},
            device_id_type=MESH,
        )

    def attend(owner):
        outputs = []
        for head in range(heads):
            query = queries[head, owner]
            peak = None
            for start in range(0, tok_all, chunk):
                cut = pl.ds(start, chunk)
                block = jnp.dot(query, keys_t[head, :, cut], preferred_element_type=F32)
                scores[head, :, cut] = block
                for at in range(0, chunk, LANES):
                    piece = block[:, at : at + LANES]
                    peak = piece if peak is None else jnp.maximum(peak, piece)
            peak = jnp.max(peak, axis=1, keepdims=True)
            for start in range(0, tok_all, chunk):
                cut = pl.ds(start, chunk)
                probs[head, :, cut] = jnp.exp2(scores[head, :, cut] - peak).astype(BF16)
            summed = jnp.dot(probs[head], values[head], preferred_element_type=F32)
            outputs.append(jnp.where(alive, summed / summed[:, HD : HD + 1], 0.0))
        pair = jnp.where(lane < HD, outputs[0], pltpu.roll(outputs[1], HD, 1))
        single, turned = outputs[2], pltpu.roll(outputs[2], HD, 1)
        low = lane[:half] < HD
        mixed = jnp.where(
            seq == 0,
            jnp.where(low, single[:half], turned[half:]),
            jnp.where(low, single[half:], turned[:half]),
        )
        return pair.astype(BF16), mixed.astype(BF16)

    def attend_send(step, carry):
        owner = lax.rem(me + step, dev_n)
        pair, mixed = attend(owner)
        parcel[owner, pl.ds(0, tok)] = pair
        parcel[owner, pl.ds(tok, half)] = mixed
        parcel_copy(owner, me).start()
        return carry

    def parcel_wait(step, carry):
        peer = lax.rem(me + step, dev_n)
        parcel_copy(peer, peer).wait()
        return carry

    lax.fori_loop(1, dev_n, attend_send, 0)
    pair, mixed = attend(me)
    landed[me, pl.ds(0, tok)] = pair
    landed[me, pl.ds(tok, half)] = mixed
    lax.fori_loop(1, dev_n, parcel_wait, 0)

    low = lane_ids(half) < HD
    for couple in range(enc_n):
        first, second = seq_n * couple, seq_n * couple + 1
        base = couple * 3 * LANES
        out[:, pl.ds(base, LANES)] = landed[first, pl.ds(0, tok)]
        out[:, pl.ds(base + 2 * LANES, LANES)] = landed[second, pl.ds(0, tok)]
        ahead = landed[first, pl.ds(tok, half)].astype(F32)
        behind = landed[second, pl.ds(tok, half)].astype(F32)
        out[pl.ds(0, half), pl.ds(base + LANES, LANES)] = jnp.where(low, ahead, behind).astype(BF16)
        out[pl.ds(half, half), pl.ds(base + LANES, LANES)] = pltpu.roll(
            jnp.where(low, behind, ahead), HD, 1
        ).astype(BF16)


def local(dims, features, conv_weight, latent_weight, lengths, clip_order, embed_weight, qkv_weight):
    enc_n, grp_n, seq_n = dims
    dev_n = enc_n * seq_n
    _, frames, rows_y, tile_w, channels = features.shape
    depth, _, cols = qkv_weight.shape
    heads = cols // HD
    half = frames * tile_w // 2
    half_all = dev_n * half
    tok = 2 * half
    span = ((rows_y - 1) * (tile_w + 2) + tile_w) * frames
    line = (tile_w + 2) * frames
    full = (rows_y + 2) * line
    feat = features[0].transpose(1, 2, 0, 3).astype(F32)
    any_space = pl.BlockSpec(memory_space=pl.ANY)
    vmem = pl.BlockSpec(memory_space=pltpu.VMEM)
    smem = pl.BlockSpec(memory_space=pltpu.SMEM)
    dma = pltpu.SemaphoreType.DMA
    result = pl.pallas_call(
        functools.partial(kernel, dims),
        out_shape=jax.ShapeDtypeStruct((tok, dev_n * cols), BF16),
        in_specs=[vmem, any_space, vmem, smem, smem, any_space, any_space],
        out_specs=vmem,
        scratch_shapes=[
            pltpu.VMEM((27, channels, channels), BF16),
            pltpu.VMEM((2 * HD, depth), BF16),
            pltpu.VMEM((3 * cols, depth), BF16),
            pltpu.VMEM((tile_w * frames, channels), BF16),
            pltpu.VMEM((2, rows_y * frames, channels), BF16),
            pltpu.VMEM((tile_w * frames, channels), BF16),
            pltpu.VMEM((2, rows_y * frames, channels), BF16),
            pltpu.VMEM((2, 2 * frames, channels), BF16),
            pltpu.VMEM((full, channels), F32),
            pltpu.VMEM((full, 3 * channels), BF16),
            pltpu.VMEM((2 * line + span, 3 * channels), BF16),
            pltpu.VMEM((half, LANES), BF16),
            pltpu.VMEM((grp_n, half, LANES), BF16),
            pltpu.VMEM((half, LANES), BF16),
            pltpu.VMEM((dev_n, half, LANES), BF16),
            pltpu.VMEM((half_all, 2 * LANES), BF16),
            pltpu.VMEM((half_all, 2 * LANES), BF16),
            pltpu.VMEM((2, 3 * cols, 2 * LANES), BF16),
            pltpu.VMEM((2, heads, LANES, 2 * LANES), BF16),
            pltpu.VMEM((2, heads, LANES, 2 * LANES), BF16),
            pltpu.VMEM((2, heads, LANES, 2 * LANES), BF16),
            pltpu.VMEM((heads, dev_n, tok, LANES), BF16),
            pltpu.VMEM((heads, LANES, 2 * half_all), BF16),
            pltpu.VMEM((heads, 2 * half_all, LANES), BF16),
            pltpu.VMEM((heads, tok, 2 * half_all), F32),
            pltpu.VMEM((heads, tok, 2 * half_all), BF16),
            pltpu.VMEM((dev_n, tok + half, LANES), BF16),
            pltpu.VMEM((dev_n, tok + half, LANES), BF16),
            dma((4,)),
            dma((5,)),
            dma((5,)),
            dma((grp_n,)),
            dma((grp_n,)),
            dma((dev_n,)),
            dma((dev_n,)),
            dma((dev_n,)),
            dma((dev_n,)),
        ],
        compiler_params=pltpu.CompilerParams(
            collective_id=0, has_side_effects=True, vmem_limit_bytes=56 * 1024 * 1024
        ),
    )(
        feat,
        conv_weight.reshape(27, channels, channels),
        latent_weight.T,
        lengths,
        clip_order,
        embed_weight,
        qkv_weight.transpose(1, 2, 0).reshape(3 * cols, depth),
    )
    result = result.reshape(rows_y // 2, tile_w // 2, frames, dev_n * cols)
    return result.transpose(2, 0, 1, 3)[None]


def solution(mesh):
    dims = (mesh.shape["enc"], mesh.shape["grp"], mesh.shape["seq"])
    placed = (
        P("grp", None, "seq", "enc", None),
        P(),
        P(),
        P(),
        P(),
        P(),
        P(None, None, ("enc", "seq")),
    )
    return jax.shard_map(
        functools.partial(local, dims),
        mesh=mesh,
        in_specs=placed,
        out_specs=P("grp", None, "seq", "enc", None),
        check_vma=False,
    )
```

```python
import functools
import math

import jax
import jax.numpy as jnp
from jax import lax
from jax.experimental import pallas as pl
from jax.experimental.pallas import tpu as pltpu
from jax.sharding import PartitionSpec as P

HD = 64
LANES = 128
MESH = pl.DeviceIdType.MESH
F32 = jnp.float32
BF16 = jnp.bfloat16
NT = (((1,), (1,)), ((), ()))


def dot_nt(a, b):
    return lax.dot_general(a, b, NT, preferred_element_type=F32)


def lane_ids(rows):
    return lax.broadcasted_iota(jnp.int32, (rows, LANES), 1)


def silu(v):
    return (v / (1.0 + jnp.exp(-v))).astype(BF16)


def kernel(
    dims,
    feat,
    conv_hbm,
    lat_w,
    lengths,
    order,
    emb_hbm,
    qkv_hbm,
    out,
    conv_w,
    emb,
    qkv,
    row_out,
    col_out,
    row_in,
    col_in,
    corner_in,
    padded,
    even,
    odd,
    patch,
    pool,
    chosen,
    gathered,
    tokens,
    key_tokens,
    wide,
    wq,
    wk,
    wv,
    queries,
    keys,
    values_t,
    scores,
    parcel,
    landed,
    load_sem,
    halo_send,
    halo_recv,
    pool_send,
    pool_recv,
    gather_send,
    gather_recv,
    parcel_send,
    parcel_recv,
):
    enc_n, grp_n, seq_n = dims
    dev_n = enc_n * seq_n
    enc, grp, seq = lax.axis_index("enc"), lax.axis_index("grp"), lax.axis_index("seq")
    me = enc * seq_n + seq
    other = 1 - seq
    rows_y, tile_w, frames, channels = feat.shape
    wide_x = tile_w + 2
    half = patch.shape[0]
    half_all = dev_n * half
    tok_all = 2 * half_all

    loads = []
    for slot, (src, dst) in enumerate(
        (
            (conv_hbm, conv_w),
            (qkv_hbm, qkv),
            (emb_hbm, emb.at[pl.ds(0, HD)]),
            (emb_hbm, emb.at[pl.ds(HD, HD)]),
        )
    ):
        copy = pltpu.make_async_copy(src, dst, load_sem.at[slot])
        copy.start()
        loads.append(copy)

    barrier = pltpu.get_barrier_semaphore()

    def greet_clip(step, carry):
        peer = lax.rem(me + step, dev_n)
        pl.semaphore_signal(
            barrier,
            inc=1,
            device_id={"enc": peer // seq_n, "seq": lax.rem(peer, seq_n)},
            device_id_type=MESH,
        )
        return carry

    def greet_pool(step, carry):
        pl.semaphore_signal(
            barrier,
            inc=1,
            device_id={"grp": lax.rem(grp + step, grp_n)},
            device_id_type=MESH,
        )
        return carry

    lax.fori_loop(1, dev_n, greet_clip, 0)
    lax.fori_loop(1, grp_n, greet_pool, 0)

    edge_y = jnp.where(seq == 0, rows_y - 1, 0)
    row_out[...] = silu(feat[edge_y].reshape(tile_w * frames, channels))
    for side, x in enumerate((0, tile_w - 1)):
        col_out[side] = silu(feat[:, x].reshape(rows_y * frames, channels))
    pl.semaphore_wait(barrier, dev_n - 1 + grp_n - 1)
    left, right = lax.rem(enc + enc_n - 1, enc_n), lax.rem(enc + 1, enc_n)
    corner = 2 * frames
    corner_from = pl.multiple_of(jnp.where(seq == 0, rows_y * frames - corner, 0), corner)
    halos = [
        pltpu.make_async_remote_copy(
            src_ref=row_out,
            dst_ref=row_in,
            send_sem=halo_send.at[0],
            recv_sem=halo_recv.at[0],
            device_id={"seq": other},
            device_id_type=MESH,
        )
    ]
    for side, target in enumerate((left, right)):
        halos.append(
            pltpu.make_async_remote_copy(
                src_ref=col_out.at[side],
                dst_ref=col_in.at[1 - side],
                send_sem=halo_send.at[1 + side],
                recv_sem=halo_recv.at[1 + side],
                device_id={"enc": target},
                device_id_type=MESH,
            )
        )
        halos.append(
            pltpu.make_async_remote_copy(
                src_ref=col_out.at[side, pl.ds(corner_from, corner)],
                dst_ref=corner_in.at[1 - side],
                send_sem=halo_send.at[3 + side],
                recv_sem=halo_recv.at[3 + side],
                device_id={"enc": target, "seq": other},
                device_id_type=MESH,
            )
        )
    for copy in halos:
        copy.start()

    line = wide_x * frames

    def place(y, x, value):
        start = (y * wide_x + x) * frames
        padded[pl.ds(start, value.shape[0])] = value

    for y in range(rows_y):
        inner = silu(feat[y].reshape(tile_w * frames, channels)).astype(F32)
        place(y + 1, 1, inner)

    for copy in loads[1:]:
        copy.wait()
    folded = dot_nt(qkv[...], emb[...])
    high = folded.astype(BF16).astype(F32)
    low = folded - high
    lane = lane_ids(folded.shape[0])
    for part in range(2):
        keep = (lane >= HD) if part else (lane < HD)
        wide[part, :, pl.ds(0, LANES)] = jnp.where(keep, high, 0.0).astype(BF16)
        wide[part, :, pl.ds(LANES, LANES)] = jnp.where(keep, low, 0.0).astype(BF16)
    heads = qkv.shape[0] // 3 // HD
    for part in range(2):
        for place_h in range(heads):
            source_h = lax.rem(place_h + seq, heads)
            for which, dst in enumerate((wq, wk, wv)):
                start = pl.multiple_of((which * heads + source_h) * HD, HD)
                block = wide[part, pl.ds(start, HD)]
                dst[part, place_h, pl.ds(0, HD)] = block
                dst[part, place_h, pl.ds(HD, HD)] = (
                    jnp.zeros_like(block) if which == 2 else block
                )

    for copy in halos:
        copy.wait()
    row = row_in[...].astype(F32)
    place(0, 1, jnp.where(seq == 1, row, 0.0))
    place(rows_y + 1, 1, jnp.where(seq == 0, row, 0.0))
    for side, x in enumerate((0, wide_x - 1)):
        present = (enc > 0) if side == 0 else (enc < enc_n - 1)
        column = jnp.where(present, col_in[side].astype(F32), 0.0)
        for y in range(rows_y):
            place(y + 1, x, column[y * frames : (y + 1) * frames])
        cells = jnp.where(present, corner_in[side].astype(F32), 0.0)
        place(0, x, jnp.where(seq == 1, cells[frames:], 0.0))
        place(rows_y + 1, x, jnp.where(seq == 0, cells[:frames], 0.0))

    frame = None
    for dst, offset in ((even, 0), (odd, frames)):
        rows = dst.shape[0]
        cells = padded[pl.ds(offset, rows)].reshape(rows // frames, frames, channels)
        frame = lax.broadcasted_iota(jnp.int32, cells.shape, 1)
        for shift in range(3):
            back = 2 - shift
            moved = cells if back == 0 else pltpu.roll(cells, back, 1)
            moved = jnp.where(frame >= back, moved, 0.0)
            dst[:, pl.ds(shift * channels, channels)] = moved.reshape(rows, channels).astype(BF16)

    loads[0].wait()
    span = ((rows_y - 1) * wide_x + tile_w) * frames
    pre = None
    for dy in range(3):
        for dx in range(3):
            src = odd if dx == 1 else even
            start = (dy * wide_x + (dx if dx == 2 else 0)) * frames
            for dt in range(3):
                term = jnp.dot(
                    src[pl.ds(start, span), pl.ds(dt * channels, channels)],
                    conv_w[(dt * 3 + dy) * 3 + dx],
                    preferred_element_type=F32,
                )
                pre = term if pre is None else pre + term

    lat_ch = lat_w.shape[0]
    own_len = lengths[grp]
    packed = None
    for y in range(rows_y):
        body = pre[y * line : y * line + tile_w * frames] + feat[y].reshape(
            tile_w * frames, channels
        )
        body = body.reshape(tile_w // 2, 2, frames, channels)
        for b in range(2):
            hidden = body[:, b].reshape(half, channels).astype(BF16)
            first = (y * 2 + b) * lat_ch
            parts = []
            if first:
                parts.append(jnp.zeros((first, channels), BF16))
            parts.append(lat_w[...])
            if first + lat_ch < LANES:
                parts.append(jnp.zeros((LANES - first - lat_ch, channels), BF16))
            term = dot_nt(hidden, jnp.concatenate(parts, axis=0))
            packed = term if packed is None else packed + term
    frame = lax.rem(lax.broadcasted_iota(jnp.int32, (half, LANES), 0), frames)
    patch[...] = jnp.where(frame < own_len, packed, 0.0).astype(BF16)

    source = jnp.int32(0)
    for n in range(grp_n):
        source = source + jnp.where(order[n] == grp, n, 0)
    source = jnp.minimum(source, grp_n - 1)
    clip_len = lengths[source]

    def pool_copy(peer, slot):
        return pltpu.make_async_remote_copy(
            src_ref=patch,
            dst_ref=pool.at[slot],
            send_sem=pool_send.at[peer],
            recv_sem=pool_recv.at[slot],
            device_id={"grp": peer},
            device_id_type=MESH,
        )

    def pool_start(step, carry):
        pool_copy(lax.rem(grp + step, grp_n), grp).start()
        return carry

    def pool_wait(step, carry):
        peer = lax.rem(grp + step, grp_n)
        pool_copy(peer, peer).wait()
        return carry

    lax.fori_loop(1, grp_n, pool_start, 0)
    pool[grp] = patch[...]
    lax.fori_loop(1, grp_n, pool_wait, 0)
    chosen[...] = pool[source]

    def owner_at(slot):
        return lax.rem(enc + 1 + slot // 2, enc_n), lax.rem(seq + 1 + slot, 2)

    def mirror(slot):
        return 2 * lax.rem(2 * enc_n - 2 - slot // 2, enc_n) + lax.rem(slot, 2)

    def gather_copy(slot):
        owner_enc, owner_seq = owner_at(slot)
        return pltpu.make_async_remote_copy(
            src_ref=chosen,
            dst_ref=gathered.at[mirror(slot)],
            send_sem=gather_send.at[slot],
            recv_sem=gather_recv.at[mirror(slot)],
            device_id={"enc": owner_enc, "seq": owner_seq},
            device_id_type=MESH,
        )

    def gather_start(slot, carry):
        gather_copy(slot).start()
        return carry

    def gather_arrived(slot, carry):
        pltpu.make_async_remote_copy(
            src_ref=chosen,
            dst_ref=gathered.at[slot],
            send_sem=gather_send.at[slot],
            recv_sem=gather_recv.at[slot],
            device_id={"enc": owner_at(slot)[0], "seq": owner_at(slot)[1]},
            device_id_type=MESH,
        ).wait()
        return carry

    group_n = dev_n // 2
    lax.fori_loop(group_n - 2, dev_n - 2, gather_start, 0)
    lax.fori_loop(0, group_n - 2, gather_start, 0)
    gather_start(dev_n - 2, 0)
    gathered[dev_n - 1] = chosen[...]

    factor = HD**-0.5 * math.log2(math.e)
    group = group_n * half
    blocks_group = group // LANES

    def project(at):
        cells = gathered[pl.ds(at * group_n, group_n)].reshape(group, LANES)
        tokens[:, pl.ds(0, LANES)] = cells
        tokens[:, pl.ds(LANES, LANES)] = cells
        wide_cells = cells.astype(F32).reshape(group // frames, frames, LANES)
        frame = lax.broadcasted_iota(jnp.int32, wide_cells.shape, 1)
        kept = jnp.where(frame < clip_len, wide_cells, wide_cells[:, :1])
        kept = kept.reshape(group, LANES).astype(BF16)
        key_tokens[:, pl.ds(0, LANES)] = kept
        key_tokens[:, pl.ds(LANES, LANES)] = kept
        row = lax.broadcasted_iota(jnp.int32, (LANES, group), 0)
        frame = lax.rem(lax.broadcasted_iota(jnp.int32, (LANES, group), 1), frames)
        counted = jnp.where(frame < clip_len, 1.0, 0.0)
        for head in range(heads):
            for part in range(2):
                query = dot_nt(wq[part, head], tokens[...]).astype(BF16).astype(F32) * factor
                high = query.astype(BF16).astype(F32)
                pair = jnp.where(row < HD, high, query - high).astype(BF16)
                for block in range(blocks_group):
                    queries[head, at * blocks_group + block, :, pl.ds(part * LANES, LANES)] = pair[
                        :, block * LANES : (block + 1) * LANES
                    ]
                first = part * half_all + at * group
                keys[head, pl.ds(first, group)] = dot_nt(key_tokens[...], wk[part, head]).astype(
                    BF16
                )
                value = dot_nt(wv[part, head], tokens[...])
                values_t[head, :, pl.ds(first, group)] = jnp.where(
                    row == HD, counted, value
                ).astype(BF16)

    lax.fori_loop(0, group_n, gather_arrived, 0)
    project(0)
    lax.fori_loop(group_n, dev_n - 1, gather_arrived, 0)
    project(1)

    chunk = tok_all // 2
    width = 2 * LANES
    block_n = half_all // LANES

    def score(head, block, start, peak):
        cut = pl.ds(start, chunk)
        made = jnp.dot(keys[head, cut], queries[head, block], preferred_element_type=F32)
        scores[head, cut] = made
        made = jnp.max(made.reshape(chunk // 8, 8, width), axis=0)
        return made if peak is None else jnp.maximum(peak, made)

    frame = lax.rem(lax.broadcasted_iota(jnp.int32, (HD, width), 1), frames)
    alive = frame < clip_len

    def parcel_copy(slot):
        owner_enc, owner_seq = owner_at(slot)
        return pltpu.make_async_remote_copy(
            src_ref=parcel.at[:, pl.ds(pl.multiple_of(slot * half, half), half)],
            dst_ref=landed.at[me],
            send_sem=parcel_send.at[slot],
            recv_sem=parcel_recv.at[me],
            device_id={"enc": owner_enc, "seq": owner_seq},
            device_id_type=MESH,
        )

    def parcel_start(slot, carry):
        parcel_copy(slot).start()
        return carry

    def parcel_wait(slot, carry):
        owner_enc, owner_seq = owner_at(slot)
        owner = owner_enc * seq_n + owner_seq
        pltpu.make_async_remote_copy(
            src_ref=parcel.at[:, pl.ds(pl.multiple_of(slot * half, half), half)],
            dst_ref=landed.at[owner],
            send_sem=parcel_send.at[slot],
            recv_sem=parcel_recv.at[owner],
            device_id={"enc": owner_enc, "seq": owner_seq},
            device_id_type=MESH,
        ).wait()
        return carry

    def attend(block, peak):
        outputs = []
        for head in range(heads):
            top = jnp.max(peak, axis=0, keepdims=True)
            peak, summed = None, None
            if head + 1 < heads:
                next_head, next_block = head + 1, block
            else:
                next_head, next_block = 0, lax.rem(block + 1, block_n)
            for start in range(0, tok_all, chunk):
                peak = score(next_head, next_block, start, peak)
                cut = pl.ds(start, chunk)
                weight = jnp.exp2(scores[head, cut] - top).astype(BF16)
                term = jnp.dot(values_t[head, :, cut], weight, preferred_element_type=F32)
                summed = term if summed is None else summed + term
            outputs.append(jnp.where(alive, summed[:HD] / summed[HD : HD + 1], 0.0))
        rows = pl.ds(pl.multiple_of(block * LANES, LANES), LANES)
        pair = jnp.concatenate(outputs[:2], axis=0).T.astype(BF16)
        parcel[0, rows] = pair[:LANES]
        parcel[1, rows] = pair[LANES:]
        first, second = outputs[2][:, :LANES], outputs[2][:, LANES:]
        mixed = jnp.concatenate(
            [jnp.where(seq == 0, first, second), jnp.where(seq == 0, second, first)], axis=0
        )
        parcel[2, rows] = mixed.T.astype(BF16)
        lax.fori_loop(
            block * LANES // half,
            jnp.minimum((block + 1) * LANES // half, dev_n - 1),
            parcel_start,
            0,
        )
        return peak

    peak = None
    for start in range(0, tok_all, chunk):
        peak = score(0, 0, start, peak)
    lax.fori_loop(0, block_n, attend, peak)
    landed[me] = parcel[:, pl.ds((dev_n - 1) * half, half)]
    lax.fori_loop(0, dev_n - 1, parcel_wait, 0)

    low = lane_ids(half) < HD
    for couple in range(enc_n):
        first, second = seq_n * couple, seq_n * couple + 1
        base = couple * 3 * LANES
        for part in range(2):
            rows = pl.ds(part * half, half)
            out[rows, pl.ds(base, LANES)] = landed[first, part]
            out[rows, pl.ds(base + 2 * LANES, LANES)] = landed[second, part]
        ahead = landed[first, 2].astype(F32)
        behind = landed[second, 2].astype(F32)
        out[pl.ds(0, half), pl.ds(base + LANES, LANES)] = jnp.where(low, ahead, behind).astype(BF16)
        out[pl.ds(half, half), pl.ds(base + LANES, LANES)] = pltpu.roll(
            jnp.where(low, behind, ahead), HD, 1
        ).astype(BF16)


def local(dims, features, conv_weight, latent_weight, lengths, clip_order, embed_weight, qkv_weight):
    enc_n, grp_n, seq_n = dims
    dev_n = enc_n * seq_n
    _, frames, rows_y, tile_w, channels = features.shape
    depth, _, cols = qkv_weight.shape
    heads = cols // HD
    half = frames * tile_w // 2
    half_all = dev_n * half
    tok = 2 * half
    span = ((rows_y - 1) * (tile_w + 2) + tile_w) * frames
    line = (tile_w + 2) * frames
    full = (rows_y + 2) * line
    feat = features[0].transpose(1, 2, 0, 3).astype(F32)
    any_space = pl.BlockSpec(memory_space=pl.ANY)
    vmem = pl.BlockSpec(memory_space=pltpu.VMEM)
    smem = pl.BlockSpec(memory_space=pltpu.SMEM)
    dma = pltpu.SemaphoreType.DMA
    result = pl.pallas_call(
        functools.partial(kernel, dims),
        out_shape=jax.ShapeDtypeStruct((tok, dev_n * cols), BF16),
        in_specs=[vmem, any_space, vmem, smem, smem, any_space, any_space],
        out_specs=vmem,
        scratch_shapes=[
            pltpu.VMEM((27, channels, channels), BF16),
            pltpu.VMEM((2 * HD, depth), BF16),
            pltpu.VMEM((3 * cols, depth), BF16),
            pltpu.VMEM((tile_w * frames, channels), BF16),
            pltpu.VMEM((2, rows_y * frames, channels), BF16),
            pltpu.VMEM((tile_w * frames, channels), BF16),
            pltpu.VMEM((2, rows_y * frames, channels), BF16),
            pltpu.VMEM((2, 2 * frames, channels), BF16),
            pltpu.VMEM((full, channels), F32),
            pltpu.VMEM((full, 3 * channels), BF16),
            pltpu.VMEM((2 * line + span, 3 * channels), BF16),
            pltpu.VMEM((half, LANES), BF16),
            pltpu.VMEM((grp_n, half, LANES), BF16),
            pltpu.VMEM((half, LANES), BF16),
            pltpu.VMEM((dev_n, half, LANES), BF16),
            pltpu.VMEM((half_all // 2, 2 * LANES), BF16),
            pltpu.VMEM((half_all // 2, 2 * LANES), BF16),
            pltpu.VMEM((2, 3 * cols, 2 * LANES), BF16),
            pltpu.VMEM((2, heads, LANES, 2 * LANES), BF16),
            pltpu.VMEM((2, heads, LANES, 2 * LANES), BF16),
            pltpu.VMEM((2, heads, LANES, 2 * LANES), BF16),
            pltpu.VMEM((heads, half_all // LANES, LANES, 2 * LANES), BF16),
            pltpu.VMEM((heads, 2 * half_all, LANES), BF16),
            pltpu.VMEM((heads, LANES, 2 * half_all), BF16),
            pltpu.VMEM((heads, 2 * half_all, 2 * LANES), F32),
            pltpu.VMEM((3, half_all, LANES), BF16),
            pltpu.VMEM((dev_n, 3, half, LANES), BF16),
            dma((4,)),
            dma((5,)),
            dma((5,)),
            dma((grp_n,)),
            dma((grp_n,)),
            dma((dev_n,)),
            dma((dev_n,)),
            dma((dev_n,)),
            dma((dev_n,)),
        ],
        compiler_params=pltpu.CompilerParams(
            collective_id=0, has_side_effects=True, vmem_limit_bytes=56 * 1024 * 1024
        ),
    )(
        feat,
        conv_weight.reshape(27, channels, channels),
        latent_weight.T,
        lengths,
        clip_order,
        embed_weight,
        qkv_weight.transpose(1, 2, 0).reshape(3 * cols, depth),
    )
    result = result.reshape(rows_y // 2, tile_w // 2, frames, dev_n * cols)
    return result.transpose(2, 0, 1, 3)[None]


def solution(mesh):
    dims = (mesh.shape["enc"], mesh.shape["grp"], mesh.shape["seq"])
    placed = (
        P("grp", None, "seq", "enc", None),
        P(),
        P(),
        P(),
        P(),
        P(),
        P(None, None, ("enc", "seq")),
    )
    return jax.shard_map(
        functools.partial(local, dims),
        mesh=mesh,
        in_specs=placed,
        out_specs=P("grp", None, "seq", "enc", None),
        check_vma=False,
    )
```

```python
import functools
import math

import jax
import jax.numpy as jnp
from jax import lax
from jax.experimental import pallas as pl
from jax.experimental.pallas import tpu as pltpu
from jax.sharding import PartitionSpec as P

HD = 64
LANES = 128
MESH = pl.DeviceIdType.MESH
F32 = jnp.float32
BF16 = jnp.bfloat16
NT = (((1,), (1,)), ((), ()))


def dot_nt(a, b):
    return lax.dot_general(a, b, NT, preferred_element_type=F32)


def lane_ids(rows):
    return lax.broadcasted_iota(jnp.int32, (rows, LANES), 1)


def silu(v):
    return (v / (1.0 + jnp.exp(-v))).astype(BF16)


def kernel(
    dims,
    feat,
    conv_hbm,
    lat_w,
    lengths,
    order,
    emb_hbm,
    qkv_hbm,
    out,
    conv_w,
    emb,
    qkv,
    row_out,
    col_out,
    row_in,
    col_in,
    corner_in,
    padded,
    even,
    odd,
    pre,
    patch,
    pool,
    chosen,
    gathered,
    tokens,
    key_tokens,
    wide,
    wqv,
    wk,
    queries,
    keys,
    values_t,
    scores,
    parcel,
    landed,
    load_sem,
    halo_send,
    halo_recv,
    pool_send,
    pool_recv,
    gather_send,
    gather_recv,
    parcel_send,
    parcel_recv,
):
    enc_n, grp_n, seq_n = dims
    dev_n = enc_n * seq_n
    enc, grp, seq = lax.axis_index("enc"), lax.axis_index("grp"), lax.axis_index("seq")
    me = enc * seq_n + seq
    other = 1 - seq
    rows_y, tile_w, frames, channels = feat.shape
    wide_x = tile_w + 2
    half = patch.shape[0]
    half_all = dev_n * half
    tok_all = 2 * half_all

    loads = []
    for slot, (src, dst) in enumerate(
        (
            (conv_hbm, conv_w),
            (qkv_hbm, qkv),
            (emb_hbm, emb.at[pl.ds(0, HD)]),
            (emb_hbm, emb.at[pl.ds(HD, HD)]),
        )
    ):
        copy = pltpu.make_async_copy(src, dst, load_sem.at[slot])
        copy.start()
        loads.append(copy)

    barrier = pltpu.get_barrier_semaphore()

    def greet_clip(step, carry):
        peer = lax.rem(me + step, dev_n)
        pl.semaphore_signal(
            barrier,
            inc=1,
            device_id={"enc": peer // seq_n, "seq": lax.rem(peer, seq_n)},
            device_id_type=MESH,
        )
        return carry

    def greet_pool(step, carry):
        pl.semaphore_signal(
            barrier,
            inc=1,
            device_id={"grp": lax.rem(grp + step, grp_n)},
            device_id_type=MESH,
        )
        return carry

    lax.fori_loop(1, dev_n, greet_clip, 0)
    lax.fori_loop(1, grp_n, greet_pool, 0)

    edge_y = jnp.where(seq == 0, rows_y - 1, 0)
    row_out[...] = silu(feat[edge_y].reshape(tile_w * frames, channels))
    for side, x in enumerate((0, tile_w - 1)):
        col_out[side] = silu(feat[:, x].reshape(rows_y * frames, channels))
    pl.semaphore_wait(barrier, dev_n - 1 + grp_n - 1)
    left, right = lax.rem(enc + enc_n - 1, enc_n), lax.rem(enc + 1, enc_n)
    corner = 2 * frames
    corner_from = pl.multiple_of(jnp.where(seq == 0, rows_y * frames - corner, 0), corner)
    halos = [
        pltpu.make_async_remote_copy(
            src_ref=row_out,
            dst_ref=row_in,
            send_sem=halo_send.at[0],
            recv_sem=halo_recv.at[0],
            device_id={"seq": other},
            device_id_type=MESH,
        )
    ]
    for side, target in enumerate((left, right)):
        halos.append(
            pltpu.make_async_remote_copy(
                src_ref=col_out.at[side],
                dst_ref=col_in.at[1 - side],
                send_sem=halo_send.at[1 + side],
                recv_sem=halo_recv.at[1 + side],
                device_id={"enc": target},
                device_id_type=MESH,
            )
        )
        halos.append(
            pltpu.make_async_remote_copy(
                src_ref=col_out.at[side, pl.ds(corner_from, corner)],
                dst_ref=corner_in.at[1 - side],
                send_sem=halo_send.at[3 + side],
                recv_sem=halo_recv.at[3 + side],
                device_id={"enc": target, "seq": other},
                device_id_type=MESH,
            )
        )
    for copy in halos:
        copy.start()

    line = wide_x * frames

    def place(y, x, value):
        start = (y * wide_x + x) * frames
        padded[pl.ds(start, value.shape[0])] = value

    for y in range(rows_y):
        inner = silu(feat[y].reshape(tile_w * frames, channels)).astype(F32)
        place(y + 1, 1, inner)

    halos[0].wait()
    row = row_in[...].astype(F32)
    place(0, 1, jnp.where(seq == 1, row, 0.0))
    place(rows_y + 1, 1, jnp.where(seq == 0, row, 0.0))
    for y in range(rows_y + 2):
        for x in (0, wide_x - 1):
            place(y, x, jnp.zeros((frames, channels), F32))

    def three_frames(cells):
        cells = cells.reshape(cells.shape[0] // frames, frames, channels)
        frame = lax.broadcasted_iota(jnp.int32, cells.shape, 1)
        for shift in range(3):
            back = 2 - shift
            moved = cells if back == 0 else pltpu.roll(cells, back, 1)
            yield shift, jnp.where(frame >= back, moved, 0.0).reshape(-1, channels)

    for dst, offset in ((even, 0), (odd, frames)):
        for shift, moved in three_frames(padded[pl.ds(offset, dst.shape[0])]):
            dst[:, pl.ds(shift * channels, channels)] = moved.astype(BF16)

    loads[0].wait()
    span = ((rows_y - 1) * wide_x + tile_w) * frames
    total = None
    for dy in range(3):
        for dx in range(3):
            src = odd if dx == 1 else even
            start = (dy * wide_x + (dx if dx == 2 else 0)) * frames
            for dt in range(3):
                term = jnp.dot(
                    src[pl.ds(start, span), pl.ds(dt * channels, channels)],
                    conv_w[(dt * 3 + dy) * 3 + dx],
                    preferred_element_type=F32,
                )
                total = term if total is None else total + term
    pre[...] = total

    for copy in halos[1:]:
        copy.wait()
    for side, dx in enumerate((0, 2)):
        present = (enc > 0) if side == 0 else (enc < enc_n - 1)
        corner_cells = corner_in[side].astype(F32)
        above = jnp.where(seq == 1, corner_cells[frames:], 0.0)
        below = jnp.where(seq == 0, corner_cells[:frames], 0.0)
        column = jnp.concatenate([above, col_in[side].astype(F32), below], axis=0)
        column = jnp.where(present, column, 0.0)
        total = None
        for dt, moved in three_frames(column):
            for dy in range(3):
                term = jnp.dot(
                    moved[dy * frames : (dy + rows_y) * frames].astype(BF16),
                    conv_w[(dt * 3 + dy) * 3 + dx],
                    preferred_element_type=F32,
                )
                total = term if total is None else total + term
        x = 0 if side == 0 else tile_w - 1
        for y in range(rows_y):
            rows = pl.ds((y * wide_x + x) * frames, frames)
            pre[rows] = pre[rows] + total[y * frames : (y + 1) * frames]

    lat_ch = lat_w.shape[0]
    own_len = lengths[grp]
    packed = None
    for y in range(rows_y):
        body = pre[pl.ds(y * line, tile_w * frames)] + feat[y].reshape(
            tile_w * frames, channels
        )
        body = body.reshape(tile_w // 2, 2, frames, channels)
        for b in range(2):
            hidden = body[:, b].reshape(half, channels).astype(BF16)
            first = (y * 2 + b) * lat_ch
            parts = []
            if first:
                parts.append(jnp.zeros((first, channels), BF16))
            parts.append(lat_w[...])
            if first + lat_ch < LANES:
                parts.append(jnp.zeros((LANES - first - lat_ch, channels), BF16))
            term = dot_nt(hidden, jnp.concatenate(parts, axis=0))
            packed = term if packed is None else packed + term
    frame = lax.rem(lax.broadcasted_iota(jnp.int32, (half, LANES), 0), frames)
    patch[...] = jnp.where(frame < own_len, packed, 0.0).astype(BF16)

    source = jnp.int32(0)
    for n in range(grp_n):
        source = source + jnp.where(order[n] == grp, n, 0)
    source = jnp.minimum(source, grp_n - 1)
    clip_len = lengths[source]

    def pool_copy(peer, slot):
        return pltpu.make_async_remote_copy(
            src_ref=patch,
            dst_ref=pool.at[slot],
            send_sem=pool_send.at[peer],
            recv_sem=pool_recv.at[slot],
            device_id={"grp": peer},
            device_id_type=MESH,
        )

    def pool_start(step, carry):
        pool_copy(lax.rem(grp + step, grp_n), grp).start()
        return carry

    def pool_wait(step, carry):
        peer = lax.rem(grp + step, grp_n)
        pool_copy(peer, peer).wait()
        return carry

    lax.fori_loop(1, grp_n, pool_start, 0)
    pool[grp] = patch[...]

    for copy in loads[1:]:
        copy.wait()
    folded = dot_nt(qkv[...], emb[...])
    high = folded.astype(BF16).astype(F32)
    low = folded - high
    lane = lane_ids(folded.shape[0])
    for part in range(2):
        keep = (lane >= HD) if part else (lane < HD)
        wide[part, :, pl.ds(0, LANES)] = jnp.where(keep, high, 0.0).astype(BF16)
        wide[part, :, pl.ds(LANES, LANES)] = jnp.where(keep, low, 0.0).astype(BF16)
    heads = qkv.shape[0] // 3 // HD
    for part in range(2):
        for place_h in range(heads):
            source_h = lax.rem(place_h + seq, heads)

            def block(which):
                start = pl.multiple_of((which * heads + source_h) * HD, HD)
                return wide[part, pl.ds(start, HD)]

            first = 2 * place_h * LANES
            wqv[part, pl.ds(first, HD)] = block(0)
            wqv[part, pl.ds(first + HD, HD)] = block(0)
            wqv[part, pl.ds(first + 2 * HD, HD)] = block(2)
            wqv[part, pl.ds(first + 3 * HD, HD)] = jnp.zeros((HD, 2 * LANES), BF16)
            wk[part, pl.ds(place_h * LANES, HD)] = block(1)
            wk[part, pl.ds(place_h * LANES + HD, HD)] = block(1)

    lax.fori_loop(1, grp_n, pool_wait, 0)
    chosen[...] = pool[source]

    def owner_at(slot):
        return lax.rem(enc + 1 + slot // 2, enc_n), lax.rem(seq + 1 + slot, 2)

    def mirror(slot):
        return 2 * lax.rem(2 * enc_n - 2 - slot // 2, enc_n) + lax.rem(slot, 2)

    def gather_copy(slot):
        owner_enc, owner_seq = owner_at(slot)
        return pltpu.make_async_remote_copy(
            src_ref=chosen,
            dst_ref=gathered.at[mirror(slot)],
            send_sem=gather_send.at[slot],
            recv_sem=gather_recv.at[mirror(slot)],
            device_id={"enc": owner_enc, "seq": owner_seq},
            device_id_type=MESH,
        )

    def gather_start(slot, carry):
        gather_copy(slot).start()
        return carry

    def gather_arrived(slot, carry):
        pltpu.make_async_remote_copy(
            src_ref=chosen,
            dst_ref=gathered.at[slot],
            send_sem=gather_send.at[slot],
            recv_sem=gather_recv.at[slot],
            device_id={"enc": owner_at(slot)[0], "seq": owner_at(slot)[1]},
            device_id_type=MESH,
        ).wait()
        return carry

    group_n = dev_n // 2
    lax.fori_loop(group_n - 2, dev_n - 2, gather_start, 0)
    lax.fori_loop(0, group_n - 2, gather_start, 0)
    gather_start(dev_n - 2, 0)
    gathered[dev_n - 1] = chosen[...]

    factor = HD**-0.5 * math.log2(math.e)
    group = group_n * half
    blocks_group = group // LANES

    def project(at):
        cells = gathered[pl.ds(at * group_n, group_n)].reshape(group, LANES)
        tokens[:, pl.ds(0, LANES)] = cells
        tokens[:, pl.ds(LANES, LANES)] = cells
        wide_cells = cells.astype(F32).reshape(group // frames, frames, LANES)
        frame = lax.broadcasted_iota(jnp.int32, wide_cells.shape, 1)
        kept = jnp.where(frame < clip_len, wide_cells, wide_cells[:, :1])
        kept = kept.reshape(group, LANES).astype(BF16)
        key_tokens[:, pl.ds(0, LANES)] = kept
        key_tokens[:, pl.ds(LANES, LANES)] = kept
        row = lax.broadcasted_iota(jnp.int32, (LANES, group), 0)
        frame = lax.rem(lax.broadcasted_iota(jnp.int32, (LANES, group), 1), frames)
        counted = jnp.where(frame < clip_len, 1.0, 0.0)
        for part in range(2):
            first = part * half_all + at * group
            made = dot_nt(key_tokens[...], wk[part])
            for head in range(heads):
                keys[head, pl.ds(first, group)] = made[:, head * LANES : (head + 1) * LANES].astype(
                    BF16
                )
            made = dot_nt(wqv[part], tokens[...])
            for head in range(heads):
                query = made[2 * head * LANES : (2 * head + 1) * LANES]
                query = query.astype(BF16).astype(F32) * factor
                high = query.astype(BF16).astype(F32)
                pair = jnp.where(row < HD, high, query - high).astype(BF16)
                for block in range(blocks_group):
                    queries[head, at * blocks_group + block, :, pl.ds(part * LANES, LANES)] = pair[
                        :, block * LANES : (block + 1) * LANES
                    ]
                value = made[(2 * head + 1) * LANES : (2 * head + 2) * LANES]
                values_t[head, :, pl.ds(first, group)] = jnp.where(
                    row == HD, counted, value
                ).astype(BF16)

    lax.fori_loop(0, group_n, gather_arrived, 0)
    project(0)
    lax.fori_loop(group_n, dev_n - 1, gather_arrived, 0)
    project(1)

    chunk = tok_all // 2
    width = 2 * LANES
    block_n = half_all // LANES

    def score(head, block, start, peak):
        cut = pl.ds(start, chunk)
        made = jnp.dot(keys[head, cut], queries[head, block], preferred_element_type=F32)
        scores[head, cut] = made
        made = jnp.max(made.reshape(chunk // 8, 8, width), axis=0)
        return made if peak is None else jnp.maximum(peak, made)

    frame = lax.rem(lax.broadcasted_iota(jnp.int32, (HD, width), 1), frames)
    alive = frame < clip_len

    def parcel_copy(slot):
        owner_enc, owner_seq = owner_at(slot)
        return pltpu.make_async_remote_copy(
            src_ref=parcel.at[:, pl.ds(pl.multiple_of(slot * half, half), half)],
            dst_ref=landed.at[me],
            send_sem=parcel_send.at[slot],
            recv_sem=parcel_recv.at[me],
            device_id={"enc": owner_enc, "seq": owner_seq},
            device_id_type=MESH,
        )

    def parcel_start(slot, carry):
        parcel_copy(slot).start()
        return carry

    def parcel_wait(slot, carry):
        owner_enc, owner_seq = owner_at(slot)
        owner = owner_enc * seq_n + owner_seq
        pltpu.make_async_remote_copy(
            src_ref=parcel.at[:, pl.ds(pl.multiple_of(slot * half, half), half)],
            dst_ref=landed.at[owner],
            send_sem=parcel_send.at[slot],
            recv_sem=parcel_recv.at[owner],
            device_id={"enc": owner_enc, "seq": owner_seq},
            device_id_type=MESH,
        ).wait()
        return carry

    def attend(block, peak):
        outputs = []
        for head in range(heads):
            top = jnp.max(peak, axis=0, keepdims=True)
            peak, summed = None, None
            if head + 1 < heads:
                next_head, next_block = head + 1, block
            else:
                next_head, next_block = 0, lax.rem(block + 1, block_n)
            for start in range(0, tok_all, chunk):
                peak = score(next_head, next_block, start, peak)
                cut = pl.ds(start, chunk)
                weight = jnp.exp2(scores[head, cut] - top).astype(BF16)
                term = jnp.dot(values_t[head, :, cut], weight, preferred_element_type=F32)
                summed = term if summed is None else summed + term
            outputs.append(jnp.where(alive, summed[:HD] / summed[HD : HD + 1], 0.0))
        rows = pl.ds(pl.multiple_of(block * LANES, LANES), LANES)
        pair = jnp.concatenate(outputs[:2], axis=0).T.astype(BF16)
        parcel[0, rows] = pair[:LANES]
        parcel[1, rows] = pair[LANES:]
        first, second = outputs[2][:, :LANES], outputs[2][:, LANES:]
        mixed = jnp.concatenate(
            [jnp.where(seq == 0, first, second), jnp.where(seq == 0, second, first)], axis=0
        )
        parcel[2, rows] = mixed.T.astype(BF16)
        lax.fori_loop(
            block * LANES // half,
            jnp.minimum((block + 1) * LANES // half, dev_n - 1),
            parcel_start,
            0,
        )
        return peak

    peak = None
    for start in range(0, tok_all, chunk):
        peak = score(0, 0, start, peak)
    lax.fori_loop(0, block_n, attend, peak)
    landed[me] = parcel[:, pl.ds((dev_n - 1) * half, half)]
    lax.fori_loop(0, dev_n - 1, parcel_wait, 0)

    low = lane_ids(half) < HD
    for couple in range(enc_n):
        first, second = seq_n * couple, seq_n * couple + 1
        base = couple * 3 * LANES
        for part in range(2):
            rows = pl.ds(part * half, half)
            out[rows, pl.ds(base, LANES)] = landed[first, part]
            out[rows, pl.ds(base + 2 * LANES, LANES)] = landed[second, part]
        ahead = landed[first, 2].astype(F32)
        behind = landed[second, 2].astype(F32)
        out[pl.ds(0, half), pl.ds(base + LANES, LANES)] = jnp.where(low, ahead, behind).astype(BF16)
        out[pl.ds(half, half), pl.ds(base + LANES, LANES)] = pltpu.roll(
            jnp.where(low, behind, ahead), HD, 1
        ).astype(BF16)


def local(dims, features, conv_weight, latent_weight, lengths, clip_order, embed_weight, qkv_weight):
    enc_n, grp_n, seq_n = dims
    dev_n = enc_n * seq_n
    _, frames, rows_y, tile_w, channels = features.shape
    depth, _, cols = qkv_weight.shape
    heads = cols // HD
    half = frames * tile_w // 2
    half_all = dev_n * half
    tok = 2 * half
    span = ((rows_y - 1) * (tile_w + 2) + tile_w) * frames
    line = (tile_w + 2) * frames
    full = (rows_y + 2) * line
    feat = features[0].transpose(1, 2, 0, 3).astype(F32)
    any_space = pl.BlockSpec(memory_space=pl.ANY)
    vmem = pl.BlockSpec(memory_space=pltpu.VMEM)
    smem = pl.BlockSpec(memory_space=pltpu.SMEM)
    dma = pltpu.SemaphoreType.DMA
    result = pl.pallas_call(
        functools.partial(kernel, dims),
        out_shape=jax.ShapeDtypeStruct((tok, dev_n * cols), BF16),
        in_specs=[vmem, any_space, vmem, smem, smem, any_space, any_space],
        out_specs=vmem,
        scratch_shapes=[
            pltpu.VMEM((27, channels, channels), BF16),
            pltpu.VMEM((2 * HD, depth), BF16),
            pltpu.VMEM((3 * cols, depth), BF16),
            pltpu.VMEM((tile_w * frames, channels), BF16),
            pltpu.VMEM((2, rows_y * frames, channels), BF16),
            pltpu.VMEM((tile_w * frames, channels), BF16),
            pltpu.VMEM((2, rows_y * frames, channels), BF16),
            pltpu.VMEM((2, 2 * frames, channels), BF16),
            pltpu.VMEM((full, channels), F32),
            pltpu.VMEM((full, 3 * channels), BF16),
            pltpu.VMEM((2 * line + span, 3 * channels), BF16),
            pltpu.VMEM((span, channels), F32),
            pltpu.VMEM((half, LANES), BF16),
            pltpu.VMEM((grp_n, half, LANES), BF16),
            pltpu.VMEM((half, LANES), BF16),
            pltpu.VMEM((dev_n, half, LANES), BF16),
            pltpu.VMEM((half_all // 2, 2 * LANES), BF16),
            pltpu.VMEM((half_all // 2, 2 * LANES), BF16),
            pltpu.VMEM((2, 3 * cols, 2 * LANES), BF16),
            pltpu.VMEM((2, 2 * heads * LANES, 2 * LANES), BF16),
            pltpu.VMEM((2, heads * LANES, 2 * LANES), BF16),
            pltpu.VMEM((heads, half_all // LANES, LANES, 2 * LANES), BF16),
            pltpu.VMEM((heads, 2 * half_all, LANES), BF16),
            pltpu.VMEM((heads, LANES, 2 * half_all), BF16),
            pltpu.VMEM((heads, 2 * half_all, 2 * LANES), F32),
            pltpu.VMEM((3, half_all, LANES), BF16),
            pltpu.VMEM((dev_n, 3, half, LANES), BF16),
            dma((4,)),
            dma((5,)),
            dma((5,)),
            dma((grp_n,)),
            dma((grp_n,)),
            dma((dev_n,)),
            dma((dev_n,)),
            dma((dev_n,)),
            dma((dev_n,)),
        ],
        compiler_params=pltpu.CompilerParams(
            collective_id=0, has_side_effects=True, vmem_limit_bytes=56 * 1024 * 1024
        ),
    )(
        feat,
        conv_weight.reshape(27, channels, channels),
        latent_weight.T,
        lengths,
        clip_order,
        embed_weight,
        qkv_weight.transpose(1, 2, 0).reshape(3 * cols, depth),
    )
    result = result.reshape(rows_y // 2, tile_w // 2, frames, dev_n * cols)
    return result.transpose(2, 0, 1, 3)[None]


def solution(mesh):
    dims = (mesh.shape["enc"], mesh.shape["grp"], mesh.shape["seq"])
    placed = (
        P("grp", None, "seq", "enc", None),
        P(),
        P(),
        P(),
        P(),
        P(),
        P(None, None, ("enc", "seq")),
    )
    return jax.shard_map(
        functools.partial(local, dims),
        mesh=mesh,
        in_specs=placed,
        out_specs=P("grp", None, "seq", "enc", None),
        check_vma=False,
    )
```

```python
import functools
import math

import jax
import jax.numpy as jnp
from jax import lax
from jax.experimental import pallas as pl
from jax.experimental.pallas import tpu as pltpu
from jax.sharding import PartitionSpec as P

HD = 64
LANES = 128
MESH = pl.DeviceIdType.MESH
F32 = jnp.float32
BF16 = jnp.bfloat16
NT = (((1,), (1,)), ((), ()))


def dot_nt(a, b):
    return lax.dot_general(a, b, NT, preferred_element_type=F32)


def lane_ids(rows):
    return lax.broadcasted_iota(jnp.int32, (rows, LANES), 1)


def silu(v):
    return (v / (1.0 + jnp.exp(-v))).astype(BF16)


def kernel(
    dims,
    feat_hbm,
    conv_hbm,
    lat_hbm,
    lengths_hbm,
    order_hbm,
    emb_hbm,
    qkv_hbm,
    out,
    raw,
    feat,
    lat_w,
    lengths,
    order,
    conv_w,
    emb,
    qkv,
    row_out,
    col_out,
    row_in,
    col_in,
    corner_in,
    padded,
    even,
    odd,
    pre,
    patch,
    pool,
    chosen,
    gathered,
    tokens,
    key_tokens,
    wide,
    wqv,
    wk,
    queries,
    keys,
    values_t,
    scores,
    parcel,
    landed,
    load_sem,
    halo_send,
    halo_recv,
    pool_send,
    pool_recv,
    gather_send,
    gather_recv,
    parcel_send,
    parcel_recv,
):
    enc_n, grp_n, seq_n = dims
    dev_n = enc_n * seq_n
    enc, grp, seq = lax.axis_index("enc"), lax.axis_index("grp"), lax.axis_index("seq")
    me = enc * seq_n + seq
    other = 1 - seq
    rows_y, tile_w, frames, channels = feat.shape
    wide_x = tile_w + 2
    half = patch.shape[0]
    half_all = dev_n * half
    tok_all = 2 * half_all

    barrier = pltpu.get_barrier_semaphore()

    def greet_clip(step, carry):
        peer = lax.rem(me + step, dev_n)
        pl.semaphore_signal(
            barrier,
            inc=1,
            device_id={"enc": peer // seq_n, "seq": lax.rem(peer, seq_n)},
            device_id_type=MESH,
        )
        return carry

    def greet_pool(step, carry):
        pl.semaphore_signal(
            barrier,
            inc=1,
            device_id={"grp": lax.rem(grp + step, grp_n)},
            device_id_type=MESH,
        )
        return carry

    lax.fori_loop(1, dev_n, greet_clip, 0)
    lax.fori_loop(1, grp_n, greet_pool, 0)

    loads = []
    for slot, (src, dst) in enumerate(
        (
            (feat_hbm, raw),
            (conv_hbm, conv_w),
            (qkv_hbm, qkv),
            (emb_hbm, emb.at[pl.ds(0, HD)]),
            (emb_hbm, emb.at[pl.ds(HD, HD)]),
            (lat_hbm, lat_w),
            (lengths_hbm, lengths),
            (order_hbm, order),
        )
    ):
        copy = pltpu.make_async_copy(src, dst, load_sem.at[slot])
        copy.start()
        loads.append(copy)

    loads[0].wait()
    cells = raw[...].astype(F32).reshape(frames, tile_w * rows_y, channels)
    cells = jnp.swapaxes(cells, 0, 1).reshape(tile_w, rows_y, frames, channels)
    for y in range(rows_y):
        feat[y] = cells[:, y]

    edge_y = jnp.where(seq == 0, rows_y - 1, 0)
    row_out[...] = silu(feat[edge_y].reshape(tile_w * frames, channels))
    for side, x in enumerate((0, tile_w - 1)):
        col_out[side] = silu(feat[:, x].reshape(rows_y * frames, channels))
    pl.semaphore_wait(barrier, dev_n - 1 + grp_n - 1)
    left, right = lax.rem(enc + enc_n - 1, enc_n), lax.rem(enc + 1, enc_n)
    corner = 2 * frames
    corner_from = pl.multiple_of(jnp.where(seq == 0, rows_y * frames - corner, 0), corner)
    halos = [
        pltpu.make_async_remote_copy(
            src_ref=row_out,
            dst_ref=row_in,
            send_sem=halo_send.at[0],
            recv_sem=halo_recv.at[0],
            device_id={"seq": other},
            device_id_type=MESH,
        )
    ]
    for side, target in enumerate((left, right)):
        halos.append(
            pltpu.make_async_remote_copy(
                src_ref=col_out.at[side],
                dst_ref=col_in.at[1 - side],
                send_sem=halo_send.at[1 + side],
                recv_sem=halo_recv.at[1 + side],
                device_id={"enc": target},
                device_id_type=MESH,
            )
        )
        halos.append(
            pltpu.make_async_remote_copy(
                src_ref=col_out.at[side, pl.ds(corner_from, corner)],
                dst_ref=corner_in.at[1 - side],
                send_sem=halo_send.at[3 + side],
                recv_sem=halo_recv.at[3 + side],
                device_id={"enc": target, "seq": other},
                device_id_type=MESH,
            )
        )
    for copy in halos:
        copy.start()

    line = wide_x * frames

    def place(y, x, value):
        start = (y * wide_x + x) * frames
        padded[pl.ds(start, value.shape[0])] = value

    for y in range(rows_y):
        inner = silu(feat[y].reshape(tile_w * frames, channels)).astype(F32)
        place(y + 1, 1, inner)

    halos[0].wait()
    row = row_in[...].astype(F32)
    place(0, 1, jnp.where(seq == 1, row, 0.0))
    place(rows_y + 1, 1, jnp.where(seq == 0, row, 0.0))
    for y in range(rows_y + 2):
        for x in (0, wide_x - 1):
            place(y, x, jnp.zeros((frames, channels), F32))

    def three_frames(cells):
        cells = cells.reshape(cells.shape[0] // frames, frames, channels)
        frame = lax.broadcasted_iota(jnp.int32, cells.shape, 1)
        for shift in range(3):
            back = 2 - shift
            moved = cells if back == 0 else pltpu.roll(cells, back, 1)
            yield shift, jnp.where(frame >= back, moved, 0.0).reshape(-1, channels)

    for dst, offset in ((even, 0), (odd, frames)):
        for shift, moved in three_frames(padded[pl.ds(offset, dst.shape[0])]):
            dst[:, pl.ds(shift * channels, channels)] = moved.astype(BF16)

    loads[1].wait()
    span = ((rows_y - 1) * wide_x + tile_w) * frames
    total = None
    for dy in range(3):
        for dx in range(3):
            src = odd if dx == 1 else even
            start = (dy * wide_x + (dx if dx == 2 else 0)) * frames
            for dt in range(3):
                term = jnp.dot(
                    src[pl.ds(start, span), pl.ds(dt * channels, channels)],
                    conv_w[(dt * 3 + dy) * 3 + dx],
                    preferred_element_type=F32,
                )
                total = term if total is None else total + term
    pre[...] = total

    for copy in halos[1:]:
        copy.wait()
    for side, dx in enumerate((0, 2)):
        present = (enc > 0) if side == 0 else (enc < enc_n - 1)
        corner_cells = corner_in[side].astype(F32)
        above = jnp.where(seq == 1, corner_cells[frames:], 0.0)
        below = jnp.where(seq == 0, corner_cells[:frames], 0.0)
        column = jnp.concatenate([above, col_in[side].astype(F32), below], axis=0)
        column = jnp.where(present, column, 0.0)
        total = None
        for dt, moved in three_frames(column):
            for dy in range(3):
                term = jnp.dot(
                    moved[dy * frames : (dy + rows_y) * frames].astype(BF16),
                    conv_w[(dt * 3 + dy) * 3 + dx],
                    preferred_element_type=F32,
                )
                total = term if total is None else total + term
        x = 0 if side == 0 else tile_w - 1
        for y in range(rows_y):
            rows = pl.ds((y * wide_x + x) * frames, frames)
            pre[rows] = pre[rows] + total[y * frames : (y + 1) * frames]

    for copy in loads[5:]:
        copy.wait()
    lat_ch = lat_w.shape[0]
    own_len = lengths[grp]
    packed = None
    for y in range(rows_y):
        body = pre[pl.ds(y * line, tile_w * frames)] + feat[y].reshape(
            tile_w * frames, channels
        )
        body = body.reshape(tile_w // 2, 2, frames, channels)
        for b in range(2):
            hidden = body[:, b].reshape(half, channels).astype(BF16)
            first = (y * 2 + b) * lat_ch
            parts = []
            if first:
                parts.append(jnp.zeros((first, channels), BF16))
            parts.append(lat_w[...])
            if first + lat_ch < LANES:
                parts.append(jnp.zeros((LANES - first - lat_ch, channels), BF16))
            term = dot_nt(hidden, jnp.concatenate(parts, axis=0))
            packed = term if packed is None else packed + term
    frame = lax.rem(lax.broadcasted_iota(jnp.int32, (half, LANES), 0), frames)
    patch[...] = jnp.where(frame < own_len, packed, 0.0).astype(BF16)

    source = jnp.int32(0)
    for n in range(grp_n):
        source = source + jnp.where(order[n] == grp, n, 0)
    source = jnp.minimum(source, grp_n - 1)
    clip_len = lengths[source]

    def pool_copy(peer, slot):
        return pltpu.make_async_remote_copy(
            src_ref=patch,
            dst_ref=pool.at[slot],
            send_sem=pool_send.at[peer],
            recv_sem=pool_recv.at[slot],
            device_id={"grp": peer},
            device_id_type=MESH,
        )

    def pool_start(step, carry):
        pool_copy(lax.rem(grp + step, grp_n), grp).start()
        return carry

    def pool_wait(step, carry):
        peer = lax.rem(grp + step, grp_n)
        pool_copy(peer, peer).wait()
        return carry

    lax.fori_loop(1, grp_n, pool_start, 0)
    pool[grp] = patch[...]

    for copy in loads[2:5]:
        copy.wait()
    folded = dot_nt(qkv[...], emb[...])
    high = folded.astype(BF16).astype(F32)
    low = folded - high
    lane = lane_ids(folded.shape[0])
    for part in range(2):
        keep = (lane >= HD) if part else (lane < HD)
        wide[part, :, pl.ds(0, LANES)] = jnp.where(keep, high, 0.0).astype(BF16)
        wide[part, :, pl.ds(LANES, LANES)] = jnp.where(keep, low, 0.0).astype(BF16)
    heads = qkv.shape[0] // 3 // HD
    for part in range(2):
        for place_h in range(heads):
            source_h = lax.rem(place_h + seq, heads)

            def block(which):
                start = pl.multiple_of((which * heads + source_h) * HD, HD)
                return wide[part, pl.ds(start, HD)]

            first = 2 * place_h * LANES
            wqv[part, pl.ds(first, HD)] = block(0)
            wqv[part, pl.ds(first + HD, HD)] = block(0)
            wqv[part, pl.ds(first + 2 * HD, HD)] = block(2)
            wqv[part, pl.ds(first + 3 * HD, HD)] = jnp.zeros((HD, 2 * LANES), BF16)
            wk[part, pl.ds(place_h * LANES, HD)] = block(1)
            wk[part, pl.ds(place_h * LANES + HD, HD)] = block(1)

    lax.fori_loop(1, grp_n, pool_wait, 0)
    chosen[...] = pool[source]

    def owner_at(slot):
        return lax.rem(enc + 1 + slot // 2, enc_n), lax.rem(seq + 1 + slot, 2)

    def mirror(slot):
        return 2 * lax.rem(2 * enc_n - 2 - slot // 2, enc_n) + lax.rem(slot, 2)

    def gather_copy(slot):
        owner_enc, owner_seq = owner_at(slot)
        return pltpu.make_async_remote_copy(
            src_ref=chosen,
            dst_ref=gathered.at[mirror(slot)],
            send_sem=gather_send.at[slot],
            recv_sem=gather_recv.at[mirror(slot)],
            device_id={"enc": owner_enc, "seq": owner_seq},
            device_id_type=MESH,
        )

    def gather_start(slot, carry):
        gather_copy(slot).start()
        return carry

    def gather_arrived(slot, carry):
        pltpu.make_async_remote_copy(
            src_ref=chosen,
            dst_ref=gathered.at[slot],
            send_sem=gather_send.at[slot],
            recv_sem=gather_recv.at[slot],
            device_id={"enc": owner_at(slot)[0], "seq": owner_at(slot)[1]},
            device_id_type=MESH,
        ).wait()
        return carry

    group_n = dev_n // 2
    lax.fori_loop(group_n - 2, dev_n - 2, gather_start, 0)
    lax.fori_loop(0, group_n - 2, gather_start, 0)
    gather_start(dev_n - 2, 0)
    gathered[dev_n - 1] = chosen[...]

    factor = HD**-0.5 * math.log2(math.e)
    group = group_n * half
    blocks_group = group // LANES

    def project(at):
        cells = gathered[pl.ds(at * group_n, group_n)].reshape(group, LANES)
        tokens[:, pl.ds(0, LANES)] = cells
        tokens[:, pl.ds(LANES, LANES)] = cells
        wide_cells = cells.astype(F32).reshape(group // frames, frames, LANES)
        frame = lax.broadcasted_iota(jnp.int32, wide_cells.shape, 1)
        kept = jnp.where(frame < clip_len, wide_cells, wide_cells[:, :1])
        kept = kept.reshape(group, LANES).astype(BF16)
        key_tokens[:, pl.ds(0, LANES)] = kept
        key_tokens[:, pl.ds(LANES, LANES)] = kept
        row = lax.broadcasted_iota(jnp.int32, (LANES, group), 0)
        frame = lax.rem(lax.broadcasted_iota(jnp.int32, (LANES, group), 1), frames)
        counted = jnp.where(frame < clip_len, 1.0, 0.0)
        for part in range(2):
            first = part * half_all + at * group
            made = dot_nt(key_tokens[...], wk[part])
            for head in range(heads):
                keys[head, pl.ds(first, group)] = made[:, head * LANES : (head + 1) * LANES].astype(
                    BF16
                )
            made = dot_nt(wqv[part], tokens[...])
            for head in range(heads):
                query = made[2 * head * LANES : (2 * head + 1) * LANES]
                query = query.astype(BF16).astype(F32) * factor
                high = query.astype(BF16).astype(F32)
                pair = jnp.where(row < HD, high, query - high).astype(BF16)
                for block in range(blocks_group):
                    queries[head, at * blocks_group + block, :, pl.ds(part * LANES, LANES)] = pair[
                        :, block * LANES : (block + 1) * LANES
                    ]
                value = made[(2 * head + 1) * LANES : (2 * head + 2) * LANES]
                values_t[head, :, pl.ds(first, group)] = jnp.where(
                    row == HD, counted, value
                ).astype(BF16)

    lax.fori_loop(0, group_n, gather_arrived, 0)
    project(0)
    lax.fori_loop(group_n, dev_n - 1, gather_arrived, 0)
    project(1)

    chunk = tok_all // 2
    width = 2 * LANES
    block_n = half_all // LANES

    def score(head, block, start, peak):
        cut = pl.ds(start, chunk)
        made = jnp.dot(keys[head, cut], queries[head, block], preferred_element_type=F32)
        scores[head, cut] = made
        made = jnp.max(made.reshape(chunk // 8, 8, width), axis=0)
        return made if peak is None else jnp.maximum(peak, made)

    frame = lax.rem(lax.broadcasted_iota(jnp.int32, (HD, width), 1), frames)
    alive = frame < clip_len

    def parcel_copy(slot):
        owner_enc, owner_seq = owner_at(slot)
        return pltpu.make_async_remote_copy(
            src_ref=parcel.at[:, pl.ds(pl.multiple_of(slot * half, half), half)],
            dst_ref=landed.at[me],
            send_sem=parcel_send.at[slot],
            recv_sem=parcel_recv.at[me],
            device_id={"enc": owner_enc, "seq": owner_seq},
            device_id_type=MESH,
        )

    def parcel_start(slot, carry):
        parcel_copy(slot).start()
        return carry

    def parcel_wait(slot, carry):
        owner_enc, owner_seq = owner_at(slot)
        owner = owner_enc * seq_n + owner_seq
        pltpu.make_async_remote_copy(
            src_ref=parcel.at[:, pl.ds(pl.multiple_of(slot * half, half), half)],
            dst_ref=landed.at[owner],
            send_sem=parcel_send.at[slot],
            recv_sem=parcel_recv.at[owner],
            device_id={"enc": owner_enc, "seq": owner_seq},
            device_id_type=MESH,
        ).wait()
        return carry

    def attend(block, peak):
        outputs = []
        for head in range(heads):
            top = jnp.max(peak, axis=0, keepdims=True)
            peak, summed = None, None
            if head + 1 < heads:
                next_head, next_block = head + 1, block
            else:
                next_head, next_block = 0, lax.rem(block + 1, block_n)
            for start in range(0, tok_all, chunk):
                peak = score(next_head, next_block, start, peak)
                cut = pl.ds(start, chunk)
                weight = jnp.exp2(scores[head, cut] - top).astype(BF16)
                term = jnp.dot(values_t[head, :, cut], weight, preferred_element_type=F32)
                summed = term if summed is None else summed + term
            outputs.append(jnp.where(alive, summed[:HD] / summed[HD : HD + 1], 0.0))
        rows = pl.ds(pl.multiple_of(block * LANES, LANES), LANES)
        pair = jnp.concatenate(outputs[:2], axis=0).T.astype(BF16)
        parcel[0, rows] = pair[:LANES]
        parcel[1, rows] = pair[LANES:]
        first, second = outputs[2][:, :LANES], outputs[2][:, LANES:]
        mixed = jnp.concatenate(
            [jnp.where(seq == 0, first, second), jnp.where(seq == 0, second, first)], axis=0
        )
        parcel[2, rows] = mixed.T.astype(BF16)
        lax.fori_loop(
            block * LANES // half,
            jnp.minimum((block + 1) * LANES // half, dev_n - 1),
            parcel_start,
            0,
        )
        return peak

    peak = None
    for start in range(0, tok_all, chunk):
        peak = score(0, 0, start, peak)
    lax.fori_loop(0, block_n, attend, peak)
    landed[me] = parcel[:, pl.ds((dev_n - 1) * half, half)]
    lax.fori_loop(0, dev_n - 1, parcel_wait, 0)

    low = lane_ids(half) < HD
    for couple in range(enc_n):
        first, second = seq_n * couple, seq_n * couple + 1
        base = couple * 3 * LANES
        for part in range(2):
            rows = pl.ds(part * half, half)
            out[rows, pl.ds(base, LANES)] = landed[first, part]
            out[rows, pl.ds(base + 2 * LANES, LANES)] = landed[second, part]
        ahead = landed[first, 2].astype(F32)
        behind = landed[second, 2].astype(F32)
        out[pl.ds(0, half), pl.ds(base + LANES, LANES)] = jnp.where(low, ahead, behind).astype(BF16)
        out[pl.ds(half, half), pl.ds(base + LANES, LANES)] = pltpu.roll(
            jnp.where(low, behind, ahead), HD, 1
        ).astype(BF16)


def local(dims, features, conv_weight, latent_weight, lengths, clip_order, embed_weight, qkv_weight):
    enc_n, grp_n, seq_n = dims
    dev_n = enc_n * seq_n
    _, frames, rows_y, tile_w, channels = features.shape
    depth, _, cols = qkv_weight.shape
    heads = cols // HD
    half = frames * tile_w // 2
    half_all = dev_n * half
    tok = 2 * half
    span = ((rows_y - 1) * (tile_w + 2) + tile_w) * frames
    line = (tile_w + 2) * frames
    full = (rows_y + 2) * line
    any_space = pl.BlockSpec(memory_space=pl.ANY)
    vmem = pl.BlockSpec(memory_space=pltpu.VMEM)
    dma = pltpu.SemaphoreType.DMA
    result = pl.pallas_call(
        functools.partial(kernel, dims),
        out_shape=jax.ShapeDtypeStruct((tok, dev_n * cols), BF16),
        in_specs=[any_space] * 7,
        out_specs=vmem,
        scratch_shapes=[
            pltpu.VMEM((frames, tile_w, rows_y, channels), BF16),
            pltpu.VMEM((rows_y, tile_w, frames, channels), F32),
            pltpu.VMEM(latent_weight.shape[::-1], BF16),
            pltpu.SMEM(lengths.shape, jnp.int32),
            pltpu.SMEM(clip_order.shape, jnp.int32),
            pltpu.VMEM((27, channels, channels), BF16),
            pltpu.VMEM((2 * HD, depth), BF16),
            pltpu.VMEM((3 * cols, depth), BF16),
            pltpu.VMEM((tile_w * frames, channels), BF16),
            pltpu.VMEM((2, rows_y * frames, channels), BF16),
            pltpu.VMEM((tile_w * frames, channels), BF16),
            pltpu.VMEM((2, rows_y * frames, channels), BF16),
            pltpu.VMEM((2, 2 * frames, channels), BF16),
            pltpu.VMEM((full, channels), F32),
            pltpu.VMEM((full, 3 * channels), BF16),
            pltpu.VMEM((2 * line + span, 3 * channels), BF16),
            pltpu.VMEM((span, channels), F32),
            pltpu.VMEM((half, LANES), BF16),
            pltpu.VMEM((grp_n, half, LANES), BF16),
            pltpu.VMEM((half, LANES), BF16),
            pltpu.VMEM((dev_n, half, LANES), BF16),
            pltpu.VMEM((half_all // 2, 2 * LANES), BF16),
            pltpu.VMEM((half_all // 2, 2 * LANES), BF16),
            pltpu.VMEM((2, 3 * cols, 2 * LANES), BF16),
            pltpu.VMEM((2, 2 * heads * LANES, 2 * LANES), BF16),
            pltpu.VMEM((2, heads * LANES, 2 * LANES), BF16),
            pltpu.VMEM((heads, half_all // LANES, LANES, 2 * LANES), BF16),
            pltpu.VMEM((heads, 2 * half_all, LANES), BF16),
            pltpu.VMEM((heads, LANES, 2 * half_all), BF16),
            pltpu.VMEM((heads, 2 * half_all, 2 * LANES), F32),
            pltpu.VMEM((3, half_all, LANES), BF16),
            pltpu.VMEM((dev_n, 3, half, LANES), BF16),
            dma((8,)),
            dma((5,)),
            dma((5,)),
            dma((grp_n,)),
            dma((grp_n,)),
            dma((dev_n,)),
            dma((dev_n,)),
            dma((dev_n,)),
            dma((dev_n,)),
        ],
        compiler_params=pltpu.CompilerParams(
            collective_id=0, has_side_effects=True, vmem_limit_bytes=56 * 1024 * 1024
        ),
    )(
        features[0].transpose(0, 2, 1, 3),
        conv_weight.reshape(27, channels, channels),
        latent_weight.T,
        lengths,
        clip_order,
        embed_weight,
        qkv_weight.transpose(1, 2, 0).reshape(3 * cols, depth),
    )
    result = result.reshape(rows_y // 2, tile_w // 2, frames, dev_n * cols)
    return result.transpose(2, 0, 1, 3)[None]


def solution(mesh):
    dims = (mesh.shape["enc"], mesh.shape["grp"], mesh.shape["seq"])
    placed = (
        P("grp", None, "seq", "enc", None),
        P(),
        P(),
        P(),
        P(),
        P(),
        P(None, None, ("enc", "seq")),
    )
    return jax.shard_map(
        functools.partial(local, dims),
        mesh=mesh,
        in_specs=placed,
        out_specs=P("grp", None, "seq", "enc", None),
        check_vma=False,
    )
```

```python
import functools
import math

import jax
import jax.numpy as jnp
from jax import lax
from jax.experimental import pallas as pl
from jax.experimental.pallas import tpu as pltpu
from jax.sharding import PartitionSpec as P

HD = 64
LANES = 128
MESH = pl.DeviceIdType.MESH
F32 = jnp.float32
BF16 = jnp.bfloat16
NT = (((1,), (1,)), ((), ()))


def dot_nt(a, b):
    return lax.dot_general(a, b, NT, preferred_element_type=F32)


def lane_ids(rows):
    return lax.broadcasted_iota(jnp.int32, (rows, LANES), 1)


def silu(v):
    return (v / (1.0 + jnp.exp(-v))).astype(BF16)


def kernel(
    dims,
    feat_hbm,
    conv_hbm,
    lat_hbm,
    lengths_hbm,
    order_hbm,
    emb_hbm,
    qkv_hbm,
    out,
    raw,
    feat,
    lat_w,
    lengths,
    order,
    conv_w,
    emb,
    qkv,
    row_out,
    row_in,
    col_in,
    padded,
    even,
    odd,
    pre,
    patch,
    pool,
    chosen,
    gathered,
    tokens,
    key_tokens,
    wide,
    wqv,
    wk,
    queries,
    keys,
    values_t,
    scores,
    parcel,
    landed,
    load_sem,
    halo_send,
    halo_recv,
    pool_send,
    pool_recv,
    gather_send,
    gather_recv,
    parcel_send,
    parcel_recv,
):
    enc_n, grp_n, seq_n = dims
    dev_n = enc_n * seq_n
    enc, grp, seq = lax.axis_index("enc"), lax.axis_index("grp"), lax.axis_index("seq")
    me = enc * seq_n + seq
    other = 1 - seq
    rows_y, tile_w, frames, channels = feat.shape
    wide_x = tile_w + 2
    half = patch.shape[0]
    half_all = dev_n * half
    tok_all = 2 * half_all

    barrier = pltpu.get_barrier_semaphore()

    def greet_clip(step, carry):
        peer = lax.rem(me + step, dev_n)
        pl.semaphore_signal(
            barrier,
            inc=1,
            device_id={"enc": peer // seq_n, "seq": lax.rem(peer, seq_n)},
            device_id_type=MESH,
        )
        return carry

    def greet_pool(step, carry):
        pl.semaphore_signal(
            barrier,
            inc=1,
            device_id={"grp": lax.rem(grp + step, grp_n)},
            device_id_type=MESH,
        )
        return carry

    lax.fori_loop(1, dev_n, greet_clip, 0)
    lax.fori_loop(1, grp_n, greet_pool, 0)

    loads = []
    for slot, (src, dst) in enumerate(
        (
            (feat_hbm, raw),
            (conv_hbm, conv_w),
            (qkv_hbm, qkv),
            (emb_hbm, emb.at[pl.ds(0, HD)]),
            (emb_hbm, emb.at[pl.ds(HD, HD)]),
            (lat_hbm, lat_w),
            (lengths_hbm, lengths),
            (order_hbm, order),
        )
    ):
        copy = pltpu.make_async_copy(src, dst, load_sem.at[slot])
        copy.start()
        loads.append(copy)

    pl.semaphore_wait(barrier, dev_n - 1 + grp_n - 1)
    left, right = lax.rem(enc + enc_n - 1, enc_n), lax.rem(enc + 1, enc_n)
    columns = []
    for side, (target, x) in enumerate(((left, 0), (right, tile_w - 1))):
        for across in range(2):
            columns.append(
                pltpu.make_async_remote_copy(
                    src_ref=feat_hbm.at[:, x],
                    dst_ref=col_in.at[1 - side, across],
                    send_sem=halo_send.at[2 * side + across],
                    recv_sem=halo_recv.at[2 * side + across],
                    device_id={"enc": target, "seq": other if across else seq},
                    device_id_type=MESH,
                )
            )
    for copy in columns:
        copy.start()

    loads[0].wait()
    cells = raw[...].astype(F32).reshape(frames, tile_w * rows_y, channels)
    cells = jnp.swapaxes(cells, 0, 1).reshape(tile_w, rows_y, frames, channels)
    for y in range(rows_y):
        feat[y] = cells[:, y]

    edge_y = jnp.where(seq == 0, rows_y - 1, 0)
    row_out[...] = silu(feat[edge_y].reshape(tile_w * frames, channels))
    row_copy = pltpu.make_async_remote_copy(
        src_ref=row_out,
        dst_ref=row_in,
        send_sem=halo_send.at[4],
        recv_sem=halo_recv.at[4],
        device_id={"seq": other},
        device_id_type=MESH,
    )
    row_copy.start()

    line = wide_x * frames

    def place(y, x, value):
        start = (y * wide_x + x) * frames
        padded[pl.ds(start, value.shape[0])] = value

    for y in range(rows_y):
        inner = silu(feat[y].reshape(tile_w * frames, channels)).astype(F32)
        place(y + 1, 1, inner)

    row_copy.wait()
    row = row_in[...].astype(F32)
    place(0, 1, jnp.where(seq == 1, row, 0.0))
    place(rows_y + 1, 1, jnp.where(seq == 0, row, 0.0))
    for y in range(rows_y + 2):
        for x in (0, wide_x - 1):
            place(y, x, jnp.zeros((frames, channels), F32))

    def three_frames(cells):
        cells = cells.reshape(cells.shape[0] // frames, frames, channels)
        frame = lax.broadcasted_iota(jnp.int32, cells.shape, 1)
        for shift in range(3):
            back = 2 - shift
            moved = cells if back == 0 else pltpu.roll(cells, back, 1)
            yield shift, jnp.where(frame >= back, moved, 0.0).reshape(-1, channels)

    for dst, offset in ((even, 0), (odd, frames)):
        for shift, moved in three_frames(padded[pl.ds(offset, dst.shape[0])]):
            dst[:, pl.ds(shift * channels, channels)] = moved.astype(BF16)

    loads[1].wait()
    span = ((rows_y - 1) * wide_x + tile_w) * frames
    total = None
    for dy in range(3):
        for dx in range(3):
            src = odd if dx == 1 else even
            start = (dy * wide_x + (dx if dx == 2 else 0)) * frames
            for dt in range(3):
                term = jnp.dot(
                    src[pl.ds(start, span), pl.ds(dt * channels, channels)],
                    conv_w[(dt * 3 + dy) * 3 + dx],
                    preferred_element_type=F32,
                )
                total = term if total is None else total + term
    pre[...] = total

    for copy in columns:
        copy.wait()
    for side, dx in enumerate((0, 2)):
        present = (enc > 0) if side == 0 else (enc < enc_n - 1)
        beside, corner = (
            jnp.swapaxes(silu(col_in[side, across].astype(F32)).astype(F32), 0, 1)
            for across in range(2)
        )
        above = jnp.where(seq == 1, corner[rows_y - 1], 0.0)
        below = jnp.where(seq == 0, corner[0], 0.0)
        column = jnp.concatenate(
            [above, beside.reshape(rows_y * frames, channels), below], axis=0
        )
        column = jnp.where(present, column, 0.0)
        total = None
        for dt, moved in three_frames(column):
            for dy in range(3):
                term = jnp.dot(
                    moved[dy * frames : (dy + rows_y) * frames].astype(BF16),
                    conv_w[(dt * 3 + dy) * 3 + dx],
                    preferred_element_type=F32,
                )
                total = term if total is None else total + term
        x = 0 if side == 0 else tile_w - 1
        for y in range(rows_y):
            rows = pl.ds((y * wide_x + x) * frames, frames)
            pre[rows] = pre[rows] + total[y * frames : (y + 1) * frames]

    for copy in loads[5:]:
        copy.wait()
    lat_ch = lat_w.shape[0]
    own_len = lengths[grp]
    packed = None
    for y in range(rows_y):
        body = pre[pl.ds(y * line, tile_w * frames)] + feat[y].reshape(
            tile_w * frames, channels
        )
        body = body.reshape(tile_w // 2, 2, frames, channels)
        for b in range(2):
            hidden = body[:, b].reshape(half, channels).astype(BF16)
            first = (y * 2 + b) * lat_ch
            parts = []
            if first:
                parts.append(jnp.zeros((first, channels), BF16))
            parts.append(lat_w[...])
            if first + lat_ch < LANES:
                parts.append(jnp.zeros((LANES - first - lat_ch, channels), BF16))
            term = dot_nt(hidden, jnp.concatenate(parts, axis=0))
            packed = term if packed is None else packed + term
    frame = lax.rem(lax.broadcasted_iota(jnp.int32, (half, LANES), 0), frames)
    patch[...] = jnp.where(frame < own_len, packed, 0.0).astype(BF16)

    source = jnp.int32(0)
    for n in range(grp_n):
        source = source + jnp.where(order[n] == grp, n, 0)
    source = jnp.minimum(source, grp_n - 1)
    clip_len = lengths[source]

    def pool_copy(peer, slot):
        return pltpu.make_async_remote_copy(
            src_ref=patch,
            dst_ref=pool.at[slot],
            send_sem=pool_send.at[peer],
            recv_sem=pool_recv.at[slot],
            device_id={"grp": peer},
            device_id_type=MESH,
        )

    def pool_start(step, carry):
        pool_copy(lax.rem(grp + step, grp_n), grp).start()
        return carry

    def pool_wait(step, carry):
        peer = lax.rem(grp + step, grp_n)
        pool_copy(peer, peer).wait()
        return carry

    lax.fori_loop(1, grp_n, pool_start, 0)
    pool[grp] = patch[...]

    for copy in loads[2:5]:
        copy.wait()
    folded = dot_nt(qkv[...], emb[...])
    high = folded.astype(BF16).astype(F32)
    low = folded - high
    lane = lane_ids(folded.shape[0])
    for part in range(2):
        keep = (lane >= HD) if part else (lane < HD)
        wide[part, :, pl.ds(0, LANES)] = jnp.where(keep, high, 0.0).astype(BF16)
        wide[part, :, pl.ds(LANES, LANES)] = jnp.where(keep, low, 0.0).astype(BF16)
    heads = qkv.shape[0] // 3 // HD
    for part in range(2):
        for place_h in range(heads):
            source_h = lax.rem(place_h + seq, heads)

            def block(which):
                start = pl.multiple_of((which * heads + source_h) * HD, HD)
                return wide[part, pl.ds(start, HD)]

            first = place_h * LANES
            wqv[part, pl.ds(first, HD)] = block(0)
            wqv[part, pl.ds(first + HD, HD)] = block(2)
            wk[part, pl.ds(place_h * LANES, HD)] = block(1)
            wk[part, pl.ds(place_h * LANES + HD, HD)] = block(1)

    row = lax.broadcasted_iota(jnp.int32, (HD, tok_all), 0)
    frame = lax.rem(lax.broadcasted_iota(jnp.int32, (HD, tok_all), 1), frames)
    counted = jnp.where((row == 0) & (frame < clip_len), 1.0, 0.0).astype(BF16)
    for head in range(heads):
        values_t[head, pl.ds(HD, HD)] = counted

    lax.fori_loop(1, grp_n, pool_wait, 0)
    chosen[...] = pool[source]

    def owner_at(slot):
        return lax.rem(enc + 1 + slot // 2, enc_n), lax.rem(seq + 1 + slot, 2)

    def mirror(slot):
        return 2 * lax.rem(2 * enc_n - 2 - slot // 2, enc_n) + lax.rem(slot, 2)

    def gather_copy(slot):
        owner_enc, owner_seq = owner_at(slot)
        return pltpu.make_async_remote_copy(
            src_ref=chosen,
            dst_ref=gathered.at[mirror(slot)],
            send_sem=gather_send.at[slot],
            recv_sem=gather_recv.at[mirror(slot)],
            device_id={"enc": owner_enc, "seq": owner_seq},
            device_id_type=MESH,
        )

    def gather_start(slot, carry):
        gather_copy(slot).start()
        return carry

    def gather_arrived(slot, carry):
        pltpu.make_async_remote_copy(
            src_ref=chosen,
            dst_ref=gathered.at[slot],
            send_sem=gather_send.at[slot],
            recv_sem=gather_recv.at[slot],
            device_id={"enc": owner_at(slot)[0], "seq": owner_at(slot)[1]},
            device_id_type=MESH,
        ).wait()
        return carry

    group_n = dev_n // 2
    lax.fori_loop(group_n - 2, dev_n - 2, gather_start, 0)
    lax.fori_loop(0, group_n - 2, gather_start, 0)
    gather_start(dev_n - 2, 0)
    gathered[dev_n - 1] = chosen[...]

    factor = HD**-0.5 * math.log2(math.e)
    group = group_n * half
    blocks_group = group // LANES

    def project(at):
        cells = gathered[pl.ds(at * group_n, group_n)].reshape(group, LANES)
        tokens[:, pl.ds(0, LANES)] = cells
        tokens[:, pl.ds(LANES, LANES)] = cells
        wide_cells = cells.astype(F32).reshape(group // frames, frames, LANES)
        frame = lax.broadcasted_iota(jnp.int32, wide_cells.shape, 1)
        kept = jnp.where(frame < clip_len, wide_cells, wide_cells[:, :1])
        kept = kept.reshape(group, LANES).astype(BF16)
        key_tokens[:, pl.ds(0, LANES)] = kept
        key_tokens[:, pl.ds(LANES, LANES)] = kept
        for part in range(2):
            first = part * half_all + at * group
            made = dot_nt(key_tokens[...], wk[part])
            for head in range(heads):
                keys[head, pl.ds(first, group)] = made[:, head * LANES : (head + 1) * LANES].astype(
                    BF16
                )
            made = dot_nt(wqv[part], tokens[...])
            for head in range(heads):
                query = made[head * LANES : head * LANES + HD]
                query = query.astype(BF16).astype(F32) * factor
                high = query.astype(BF16)
                low = (query - high.astype(F32)).astype(BF16)
                for block in range(blocks_group):
                    cut = slice(block * LANES, (block + 1) * LANES)
                    spot = queries.at[head, at * blocks_group + block, :, pl.ds(part * LANES, LANES)]
                    spot[pl.ds(0, HD)] = high[:, cut]
                    spot[pl.ds(HD, HD)] = low[:, cut]
                values_t[head, pl.ds(0, HD), pl.ds(first, group)] = made[
                    head * LANES + HD : (head + 1) * LANES
                ].astype(BF16)

    lax.fori_loop(0, group_n, gather_arrived, 0)
    project(0)
    lax.fori_loop(group_n, dev_n - 1, gather_arrived, 0)
    project(1)

    chunk = tok_all // 2
    width = 2 * LANES
    block_n = half_all // LANES

    def score(head, block, start, peak):
        cut = pl.ds(start, chunk)
        made = jnp.dot(keys[head, cut], queries[head, block], preferred_element_type=F32)
        scores[head, cut] = made
        made = jnp.max(made.reshape(chunk // 8, 8, width), axis=0)
        return made if peak is None else jnp.maximum(peak, made)

    frame = lax.rem(lax.broadcasted_iota(jnp.int32, (HD, width), 1), frames)
    alive = frame < clip_len

    def parcel_copy(slot):
        owner_enc, owner_seq = owner_at(slot)
        return pltpu.make_async_remote_copy(
            src_ref=parcel.at[:, pl.ds(pl.multiple_of(slot * half, half), half)],
            dst_ref=landed.at[me],
            send_sem=parcel_send.at[slot],
            recv_sem=parcel_recv.at[me],
            device_id={"enc": owner_enc, "seq": owner_seq},
            device_id_type=MESH,
        )

    def parcel_start(slot, carry):
        parcel_copy(slot).start()
        return carry

    def parcel_wait(slot, carry):
        owner_enc, owner_seq = owner_at(slot)
        owner = owner_enc * seq_n + owner_seq
        pltpu.make_async_remote_copy(
            src_ref=parcel.at[:, pl.ds(pl.multiple_of(slot * half, half), half)],
            dst_ref=landed.at[owner],
            send_sem=parcel_send.at[slot],
            recv_sem=parcel_recv.at[owner],
            device_id={"enc": owner_enc, "seq": owner_seq},
            device_id_type=MESH,
        ).wait()
        return carry

    def attend(block, peak, last=False):
        outputs = []
        for head in range(heads):
            top = jnp.max(peak, axis=0, keepdims=True)
            peak, summed = None, None
            if head + 1 < heads:
                next_head, next_block = head + 1, block
            else:
                next_head, next_block = 0, block + 1
            for start in range(0, tok_all, chunk):
                if not last or head + 1 < heads:
                    peak = score(next_head, next_block, start, peak)
                cut = pl.ds(start, chunk)
                weight = jnp.exp2(scores[head, cut] - top).astype(BF16)
                term = jnp.dot(values_t[head, :, cut], weight, preferred_element_type=F32)
                summed = term if summed is None else summed + term
            outputs.append(jnp.where(alive, summed[:HD] / summed[HD : HD + 1], 0.0))
        rows = pl.ds(pl.multiple_of(block * LANES, LANES), LANES)
        pair = jnp.concatenate(outputs[:2], axis=0).T.astype(BF16)
        parcel[0, rows] = pair[:LANES]
        parcel[1, rows] = pair[LANES:]
        first, second = outputs[2][:, :LANES], outputs[2][:, LANES:]
        mixed = jnp.concatenate(
            [jnp.where(seq == 0, first, second), jnp.where(seq == 0, second, first)], axis=0
        )
        parcel[2, rows] = mixed.T.astype(BF16)
        lax.fori_loop(
            block * LANES // half,
            jnp.minimum((block + 1) * LANES // half, dev_n - 1),
            parcel_start,
            0,
        )
        return peak

    peak = None
    for start in range(0, tok_all, chunk):
        peak = score(0, 0, start, peak)
    peak = lax.fori_loop(0, block_n - 1, attend, peak)
    attend(jnp.int32(block_n - 1), peak, last=True)
    landed[me] = parcel[:, pl.ds((dev_n - 1) * half, half)]
    lax.fori_loop(0, dev_n - 1, parcel_wait, 0)

    low = lane_ids(half) < HD
    for couple in range(enc_n):
        first, second = seq_n * couple, seq_n * couple + 1
        base = couple * 3 * LANES
        for part in range(2):
            rows = pl.ds(part * half, half)
            out[rows, pl.ds(base, LANES)] = landed[first, part]
            out[rows, pl.ds(base + 2 * LANES, LANES)] = landed[second, part]
        ahead = landed[first, 2].astype(F32)
        behind = landed[second, 2].astype(F32)
        out[pl.ds(0, half), pl.ds(base + LANES, LANES)] = jnp.where(low, ahead, behind).astype(BF16)
        out[pl.ds(half, half), pl.ds(base + LANES, LANES)] = pltpu.roll(
            jnp.where(low, behind, ahead), HD, 1
        ).astype(BF16)


def local(dims, features, conv_weight, latent_weight, lengths, clip_order, embed_weight, qkv_weight):
    enc_n, grp_n, seq_n = dims
    dev_n = enc_n * seq_n
    _, frames, rows_y, tile_w, channels = features.shape
    depth, _, cols = qkv_weight.shape
    heads = cols // HD
    half = frames * tile_w // 2
    half_all = dev_n * half
    tok = 2 * half
    span = ((rows_y - 1) * (tile_w + 2) + tile_w) * frames
    line = (tile_w + 2) * frames
    full = (rows_y + 2) * line
    in_hbm = pl.BlockSpec(memory_space=pltpu.HBM)
    vmem = pl.BlockSpec(memory_space=pltpu.VMEM)
    dma = pltpu.SemaphoreType.DMA
    result = pl.pallas_call(
        functools.partial(kernel, dims),
        out_shape=jax.ShapeDtypeStruct((tok, dev_n * cols), BF16),
        in_specs=[in_hbm] * 7,
        out_specs=vmem,
        scratch_shapes=[
            pltpu.VMEM((frames, tile_w, rows_y, channels), BF16),
            pltpu.VMEM((rows_y, tile_w, frames, channels), F32),
            pltpu.VMEM(latent_weight.shape[::-1], BF16),
            pltpu.SMEM(lengths.shape, jnp.int32),
            pltpu.SMEM(clip_order.shape, jnp.int32),
            pltpu.VMEM((27, channels, channels), BF16),
            pltpu.VMEM((2 * HD, depth), BF16),
            pltpu.VMEM((3 * cols, depth), BF16),
            pltpu.VMEM((tile_w * frames, channels), BF16),
            pltpu.VMEM((tile_w * frames, channels), BF16),
            pltpu.VMEM((2, 2, frames, rows_y, channels), BF16),
            pltpu.VMEM((full, channels), F32),
            pltpu.VMEM((full, 3 * channels), BF16),
            pltpu.VMEM((2 * line + span, 3 * channels), BF16),
            pltpu.VMEM((span, channels), F32),
            pltpu.VMEM((half, LANES), BF16),
            pltpu.VMEM((grp_n, half, LANES), BF16),
            pltpu.VMEM((half, LANES), BF16),
            pltpu.VMEM((dev_n, half, LANES), BF16),
            pltpu.VMEM((half_all // 2, 2 * LANES), BF16),
            pltpu.VMEM((half_all // 2, 2 * LANES), BF16),
            pltpu.VMEM((2, 3 * cols, 2 * LANES), BF16),
            pltpu.VMEM((2, heads * LANES, 2 * LANES), BF16),
            pltpu.VMEM((2, heads * LANES, 2 * LANES), BF16),
            pltpu.VMEM((heads, half_all // LANES, LANES, 2 * LANES), BF16),
            pltpu.VMEM((heads, 2 * half_all, LANES), BF16),
            pltpu.VMEM((heads, LANES, 2 * half_all), BF16),
            pltpu.VMEM((heads, 2 * half_all, 2 * LANES), F32),
            pltpu.VMEM((3, half_all, LANES), BF16),
            pltpu.VMEM((dev_n, 3, half, LANES), BF16),
            dma((8,)),
            dma((5,)),
            dma((5,)),
            dma((grp_n,)),
            dma((grp_n,)),
            dma((dev_n,)),
            dma((dev_n,)),
            dma((dev_n,)),
            dma((dev_n,)),
        ],
        compiler_params=pltpu.CompilerParams(
            collective_id=0, has_side_effects=True, vmem_limit_bytes=42 * 1024 * 1024
        ),
    )(
        *(
            pltpu.with_memory_space_constraint(operand, pltpu.HBM)
            for operand in (
                features[0].transpose(0, 2, 1, 3),
                conv_weight.reshape(27, channels, channels),
                latent_weight.T,
                lengths,
                clip_order,
                embed_weight,
                qkv_weight.transpose(1, 2, 0).reshape(3 * cols, depth),
            )
        )
    )
    result = result.reshape(rows_y // 2, tile_w // 2, frames, dev_n * cols)
    return result.transpose(2, 0, 1, 3)[None]


def solution(mesh):
    dims = (mesh.shape["enc"], mesh.shape["grp"], mesh.shape["seq"])
    placed = (
        P("grp", None, "seq", "enc", None),
        P(),
        P(),
        P(),
        P(),
        P(),
        P(None, None, ("enc", "seq")),
    )
    return jax.shard_map(
        functools.partial(local, dims),
        mesh=mesh,
        in_specs=placed,
        out_specs=P("grp", None, "seq", "enc", None),
        check_vma=False,
    )
```

```python
import functools
import math

import jax
import jax.numpy as jnp
from jax import lax
from jax.experimental import pallas as pl
from jax.experimental.pallas import tpu as pltpu
from jax.sharding import PartitionSpec as P

HD = 64
LANES = 128
MESH = pl.DeviceIdType.MESH
F32 = jnp.float32
BF16 = jnp.bfloat16
NT = (((1,), (1,)), ((), ()))


def dot_nt(a, b):
    return lax.dot_general(a, b, NT, preferred_element_type=F32)


def lane_ids(rows):
    return lax.broadcasted_iota(jnp.int32, (rows, LANES), 1)


def silu(v):
    return (v / (1.0 + jnp.exp(-v))).astype(BF16)


def kernel(
    dims,
    feat_hbm,
    conv_hbm,
    lat_hbm,
    lengths_hbm,
    order_hbm,
    emb_hbm,
    qkv_hbm,
    out,
    raw,
    feat,
    lat_w,
    lengths,
    order,
    conv_w,
    emb,
    qkv,
    row_out,
    row_in,
    col_in,
    padded,
    even,
    odd,
    pre,
    patch,
    pool,
    chosen,
    gathered,
    tokens,
    key_tokens,
    wide,
    wqv,
    wk,
    queries,
    keys,
    values_t,
    scores,
    parcel,
    landed,
    load_sem,
    halo_send,
    halo_recv,
    pool_send,
    pool_recv,
    gather_send,
    gather_recv,
    parcel_send,
    parcel_recv,
):
    enc_n, grp_n, seq_n = dims
    dev_n = enc_n * seq_n
    enc, grp, seq = lax.axis_index("enc"), lax.axis_index("grp"), lax.axis_index("seq")
    me = enc * seq_n + seq
    other = 1 - seq
    rows_y, tile_w, frames, channels = feat.shape
    wide_x = tile_w + 2
    half = patch.shape[0]
    half_all = dev_n * half
    tok_all = 2 * half_all

    barrier = pltpu.get_barrier_semaphore()

    def greet_clip(step, carry):
        peer = lax.rem(me + step, dev_n)
        pl.semaphore_signal(
            barrier,
            inc=1,
            device_id={"enc": peer // seq_n, "seq": lax.rem(peer, seq_n)},
            device_id_type=MESH,
        )
        return carry

    def greet_pool(step, carry):
        pl.semaphore_signal(
            barrier,
            inc=1,
            device_id={"grp": lax.rem(grp + step, grp_n)},
            device_id_type=MESH,
        )
        return carry

    lax.fori_loop(1, dev_n, greet_clip, 0)
    lax.fori_loop(1, grp_n, greet_pool, 0)

    loads = []
    for slot, (src, dst) in enumerate(
        (
            (feat_hbm, raw),
            (conv_hbm, conv_w),
            (qkv_hbm, qkv),
            (emb_hbm, emb.at[pl.ds(0, HD)]),
            (emb_hbm, emb.at[pl.ds(HD, HD)]),
            (lat_hbm, lat_w),
            (lengths_hbm, lengths),
            (order_hbm, order),
        )
    ):
        copy = pltpu.make_async_copy(src, dst, load_sem.at[slot])
        copy.start()
        loads.append(copy)

    pl.semaphore_wait(barrier, dev_n - 1 + grp_n - 1)
    left, right = lax.rem(enc + enc_n - 1, enc_n), lax.rem(enc + 1, enc_n)
    columns = []
    for side, (target, x) in enumerate(((left, 0), (right, tile_w - 1))):
        for across in range(2):
            columns.append(
                pltpu.make_async_remote_copy(
                    src_ref=feat_hbm.at[:, x],
                    dst_ref=col_in.at[1 - side, across],
                    send_sem=halo_send.at[2 * side + across],
                    recv_sem=halo_recv.at[2 * side + across],
                    device_id={"enc": target, "seq": other if across else seq},
                    device_id_type=MESH,
                )
            )
    for copy in columns:
        copy.start()

    loads[0].wait()
    cells = raw[...].astype(F32).reshape(frames, tile_w * rows_y, channels)
    cells = jnp.swapaxes(cells, 0, 1).reshape(tile_w, rows_y, frames, channels)
    for y in range(rows_y):
        feat[y] = cells[:, y]

    edge_y = jnp.where(seq == 0, rows_y - 1, 0)
    row_out[...] = silu(feat[edge_y].reshape(tile_w * frames, channels))
    row_copy = pltpu.make_async_remote_copy(
        src_ref=row_out,
        dst_ref=row_in,
        send_sem=halo_send.at[4],
        recv_sem=halo_recv.at[4],
        device_id={"seq": other},
        device_id_type=MESH,
    )
    row_copy.start()

    line = wide_x * frames

    def place(y, x, value):
        start = (y * wide_x + x) * frames
        padded[pl.ds(start, value.shape[0])] = value

    for y in range(rows_y):
        inner = silu(feat[y].reshape(tile_w * frames, channels)).astype(F32)
        place(y + 1, 1, inner)

    row_copy.wait()
    row = row_in[...].astype(F32)
    place(0, 1, jnp.where(seq == 1, row, 0.0))
    place(rows_y + 1, 1, jnp.where(seq == 0, row, 0.0))
    for y in range(rows_y + 2):
        for x in (0, wide_x - 1):
            place(y, x, jnp.zeros((frames, channels), F32))

    def three_frames(cells):
        cells = cells.reshape(cells.shape[0] // frames, frames, channels)
        frame = lax.broadcasted_iota(jnp.int32, cells.shape, 1)
        for shift in range(3):
            back = 2 - shift
            moved = cells if back == 0 else pltpu.roll(cells, back, 1)
            yield shift, jnp.where(frame >= back, moved, 0.0).reshape(-1, channels)

    for dst, offset in ((even, 0), (odd, frames)):
        for shift, moved in three_frames(padded[pl.ds(offset, dst.shape[0])]):
            dst[:, pl.ds(shift * channels, channels)] = moved.astype(BF16)

    loads[1].wait()
    span = ((rows_y - 1) * wide_x + tile_w) * frames

    def taps(dy, carry):
        total = None
        for dx in range(3):
            src = odd if dx == 1 else even
            start = pl.multiple_of((dy * wide_x + (dx if dx == 2 else 0)) * frames, 2 * frames)
            for dt in range(3):
                term = jnp.dot(
                    src[pl.ds(start, span), pl.ds(dt * channels, channels)],
                    conv_w[(dt * 3 + dy) * 3 + dx],
                    preferred_element_type=F32,
                )
                total = term if total is None else total + term
        pre[...] = pre[...] + total
        return carry

    pre[...] = jnp.zeros_like(pre)
    lax.fori_loop(0, 3, taps, 0)

    for copy in columns:
        copy.wait()
    for side, dx in enumerate((0, 2)):
        present = (enc > 0) if side == 0 else (enc < enc_n - 1)
        beside, corner = (
            jnp.swapaxes(silu(col_in[side, across].astype(F32)).astype(F32), 0, 1)
            for across in range(2)
        )
        above = jnp.where(seq == 1, corner[rows_y - 1], 0.0)
        below = jnp.where(seq == 0, corner[0], 0.0)
        column = jnp.concatenate(
            [above, beside.reshape(rows_y * frames, channels), below], axis=0
        )
        column = jnp.where(present, column, 0.0)
        total = None
        for dt, moved in three_frames(column):
            for dy in range(3):
                term = jnp.dot(
                    moved[dy * frames : (dy + rows_y) * frames].astype(BF16),
                    conv_w[(dt * 3 + dy) * 3 + dx],
                    preferred_element_type=F32,
                )
                total = term if total is None else total + term
        x = 0 if side == 0 else tile_w - 1
        for y in range(rows_y):
            rows = pl.ds((y * wide_x + x) * frames, frames)
            pre[rows] = pre[rows] + total[y * frames : (y + 1) * frames]

    for copy in loads[5:]:
        copy.wait()
    lat_ch = lat_w.shape[0]
    own_len = lengths[grp]
    packed = None
    for y in range(rows_y):
        body = pre[pl.ds(y * line, tile_w * frames)] + feat[y].reshape(
            tile_w * frames, channels
        )
        body = body.reshape(tile_w // 2, 2, frames, channels)
        for b in range(2):
            hidden = body[:, b].reshape(half, channels).astype(BF16)
            first = (y * 2 + b) * lat_ch
            parts = []
            if first:
                parts.append(jnp.zeros((first, channels), BF16))
            parts.append(lat_w[...])
            if first + lat_ch < LANES:
                parts.append(jnp.zeros((LANES - first - lat_ch, channels), BF16))
            term = dot_nt(hidden, jnp.concatenate(parts, axis=0))
            packed = term if packed is None else packed + term
    frame = lax.rem(lax.broadcasted_iota(jnp.int32, (half, LANES), 0), frames)
    patch[...] = jnp.where(frame < own_len, packed, 0.0).astype(BF16)

    source = jnp.int32(0)
    for n in range(grp_n):
        source = source + jnp.where(order[n] == grp, n, 0)
    source = jnp.minimum(source, grp_n - 1)
    clip_len = lengths[source]

    def pool_copy(peer, slot):
        return pltpu.make_async_remote_copy(
            src_ref=patch,
            dst_ref=pool.at[slot],
            send_sem=pool_send.at[peer],
            recv_sem=pool_recv.at[slot],
            device_id={"grp": peer},
            device_id_type=MESH,
        )

    def pool_start(step, carry):
        pool_copy(lax.rem(grp + step, grp_n), grp).start()
        return carry

    def pool_wait(step, carry):
        peer = lax.rem(grp + step, grp_n)
        pool_copy(peer, peer).wait()
        return carry

    lax.fori_loop(1, grp_n, pool_start, 0)
    pool[grp] = patch[...]

    for copy in loads[2:5]:
        copy.wait()
    folded = dot_nt(qkv[...], emb[...])
    high = folded.astype(BF16).astype(F32)
    low = folded - high
    lane = lane_ids(folded.shape[0])
    for part in range(2):
        keep = (lane >= HD) if part else (lane < HD)
        wide[part, :, pl.ds(0, LANES)] = jnp.where(keep, high, 0.0).astype(BF16)
        wide[part, :, pl.ds(LANES, LANES)] = jnp.where(keep, low, 0.0).astype(BF16)
    heads = qkv.shape[0] // 3 // HD
    for part in range(2):
        for place_h in range(heads):
            source_h = lax.rem(place_h + seq, heads)

            def block(which):
                start = pl.multiple_of((which * heads + source_h) * HD, HD)
                return wide[part, pl.ds(start, HD)]

            first = place_h * LANES
            wqv[part, pl.ds(first, HD)] = block(0)
            wqv[part, pl.ds(first + HD, HD)] = block(2)
            wk[part, pl.ds(place_h * LANES, HD)] = block(1)
            wk[part, pl.ds(place_h * LANES + HD, HD)] = block(1)

    row = lax.broadcasted_iota(jnp.int32, (HD, tok_all), 0)
    frame = lax.rem(lax.broadcasted_iota(jnp.int32, (HD, tok_all), 1), frames)
    counted = jnp.where((row == 0) & (frame < clip_len), 1.0, 0.0).astype(BF16)
    for head in range(heads):
        values_t[head, pl.ds(HD, HD)] = counted

    lax.fori_loop(1, grp_n, pool_wait, 0)
    chosen[...] = pool[source]

    def owner_at(slot):
        return lax.rem(enc + 1 + slot // 2, enc_n), lax.rem(seq + 1 + slot, 2)

    def mirror(slot):
        return 2 * lax.rem(2 * enc_n - 2 - slot // 2, enc_n) + lax.rem(slot, 2)

    def gather_copy(slot):
        owner_enc, owner_seq = owner_at(slot)
        return pltpu.make_async_remote_copy(
            src_ref=chosen,
            dst_ref=gathered.at[mirror(slot)],
            send_sem=gather_send.at[slot],
            recv_sem=gather_recv.at[mirror(slot)],
            device_id={"enc": owner_enc, "seq": owner_seq},
            device_id_type=MESH,
        )

    def gather_start(slot, carry):
        gather_copy(slot).start()
        return carry

    def gather_arrived(slot, carry):
        pltpu.make_async_remote_copy(
            src_ref=chosen,
            dst_ref=gathered.at[slot],
            send_sem=gather_send.at[slot],
            recv_sem=gather_recv.at[slot],
            device_id={"enc": owner_at(slot)[0], "seq": owner_at(slot)[1]},
            device_id_type=MESH,
        ).wait()
        return carry

    group_n = dev_n // 2
    lax.fori_loop(group_n - 2, dev_n - 2, gather_start, 0)
    lax.fori_loop(0, group_n - 2, gather_start, 0)
    gather_start(dev_n - 2, 0)
    gathered[dev_n - 1] = chosen[...]

    factor = HD**-0.5 * math.log2(math.e)
    group = group_n * half
    blocks_group = group // LANES

    def project(at, carry):
        lax.fori_loop(
            at * group_n, jnp.minimum((at + 1) * group_n, dev_n - 1), gather_arrived, 0
        )
        cells = gathered[pl.ds(at * group_n, group_n)].reshape(group, LANES)
        tokens[:, pl.ds(0, LANES)] = cells
        tokens[:, pl.ds(LANES, LANES)] = cells
        wide_cells = cells.astype(F32).reshape(group // frames, frames, LANES)
        frame = lax.broadcasted_iota(jnp.int32, wide_cells.shape, 1)
        kept = jnp.where(frame < clip_len, wide_cells, wide_cells[:, :1])
        kept = kept.reshape(group, LANES).astype(BF16)
        key_tokens[:, pl.ds(0, LANES)] = kept
        key_tokens[:, pl.ds(LANES, LANES)] = kept
        for part in range(2):
            first = pl.multiple_of(part * half_all + at * group, LANES)
            made = dot_nt(key_tokens[...], wk[part])
            for head in range(heads):
                keys[head, pl.ds(first, group)] = made[:, head * LANES : (head + 1) * LANES].astype(
                    BF16
                )
            made = dot_nt(wqv[part], tokens[...])
            for head in range(heads):
                query = made[head * LANES : head * LANES + HD]
                query = query.astype(BF16).astype(F32) * factor
                high = query.astype(BF16)
                low = (query - high.astype(F32)).astype(BF16)
                for block in range(blocks_group):
                    cut = slice(block * LANES, (block + 1) * LANES)
                    spot = queries.at[head, at * blocks_group + block, :, pl.ds(part * LANES, LANES)]
                    spot[pl.ds(0, HD)] = high[:, cut]
                    spot[pl.ds(HD, HD)] = low[:, cut]
                values_t[head, pl.ds(0, HD), pl.ds(first, group)] = made[
                    head * LANES + HD : (head + 1) * LANES
                ].astype(BF16)
        return carry

    lax.fori_loop(0, 2, project, 0)

    chunk = tok_all // 2
    width = 2 * LANES
    block_n = half_all // LANES

    def score(head, block, start, peak):
        cut = pl.ds(start, chunk)
        made = jnp.dot(keys[head, cut], queries[head, block], preferred_element_type=F32)
        scores[head, cut] = made
        made = jnp.max(made.reshape(chunk // 8, 8, width), axis=0)
        return made if peak is None else jnp.maximum(peak, made)

    frame = lax.rem(lax.broadcasted_iota(jnp.int32, (HD, width), 1), frames)
    alive = frame < clip_len

    def parcel_copy(slot):
        owner_enc, owner_seq = owner_at(slot)
        return pltpu.make_async_remote_copy(
            src_ref=parcel.at[:, pl.ds(pl.multiple_of(slot * half, half), half)],
            dst_ref=landed.at[me],
            send_sem=parcel_send.at[slot],
            recv_sem=parcel_recv.at[me],
            device_id={"enc": owner_enc, "seq": owner_seq},
            device_id_type=MESH,
        )

    def parcel_start(slot, carry):
        parcel_copy(slot).start()
        return carry

    def parcel_wait(slot, carry):
        owner_enc, owner_seq = owner_at(slot)
        owner = owner_enc * seq_n + owner_seq
        pltpu.make_async_remote_copy(
            src_ref=parcel.at[:, pl.ds(pl.multiple_of(slot * half, half), half)],
            dst_ref=landed.at[owner],
            send_sem=parcel_send.at[slot],
            recv_sem=parcel_recv.at[owner],
            device_id={"enc": owner_enc, "seq": owner_seq},
            device_id_type=MESH,
        ).wait()
        return carry

    def attend(block, peak):
        outputs = []
        for head in range(heads):
            top = jnp.max(peak, axis=0, keepdims=True)
            peak, summed = None, None
            if head + 1 < heads:
                next_head, next_block = head + 1, block
            else:
                next_head, next_block = 0, lax.rem(block + 1, block_n)
            for start in range(0, tok_all, chunk):
                peak = score(next_head, next_block, start, peak)
                cut = pl.ds(start, chunk)
                weight = jnp.exp2(scores[head, cut] - top).astype(BF16)
                term = jnp.dot(values_t[head, :, cut], weight, preferred_element_type=F32)
                summed = term if summed is None else summed + term
            outputs.append(jnp.where(alive, summed[:HD] / summed[HD : HD + 1], 0.0))
        rows = pl.ds(pl.multiple_of(block * LANES, LANES), LANES)
        pair = jnp.concatenate(outputs[:2], axis=0).T.astype(BF16)
        parcel[0, rows] = pair[:LANES]
        parcel[1, rows] = pair[LANES:]
        first, second = outputs[2][:, :LANES], outputs[2][:, LANES:]
        mixed = jnp.concatenate(
            [jnp.where(seq == 0, first, second), jnp.where(seq == 0, second, first)], axis=0
        )
        parcel[2, rows] = mixed.T.astype(BF16)
        lax.fori_loop(
            block * LANES // half,
            jnp.minimum((block + 1) * LANES // half, dev_n - 1),
            parcel_start,
            0,
        )
        return peak

    peak = None
    for start in range(0, tok_all, chunk):
        peak = score(0, 0, start, peak)
    lax.fori_loop(0, block_n, attend, peak)
    landed[me] = parcel[:, pl.ds((dev_n - 1) * half, half)]
    lax.fori_loop(0, dev_n - 1, parcel_wait, 0)

    low = lane_ids(half) < HD
    for couple in range(enc_n):
        first, second = seq_n * couple, seq_n * couple + 1
        base = couple * 3 * LANES
        for part in range(2):
            rows = pl.ds(part * half, half)
            out[rows, pl.ds(base, LANES)] = landed[first, part]
            out[rows, pl.ds(base + 2 * LANES, LANES)] = landed[second, part]
        ahead = landed[first, 2].astype(F32)
        behind = landed[second, 2].astype(F32)
        out[pl.ds(0, half), pl.ds(base + LANES, LANES)] = jnp.where(low, ahead, behind).astype(BF16)
        out[pl.ds(half, half), pl.ds(base + LANES, LANES)] = pltpu.roll(
            jnp.where(low, behind, ahead), HD, 1
        ).astype(BF16)


def local(dims, features, conv_weight, latent_weight, lengths, clip_order, embed_weight, qkv_weight):
    enc_n, grp_n, seq_n = dims
    dev_n = enc_n * seq_n
    _, frames, rows_y, tile_w, channels = features.shape
    depth, _, cols = qkv_weight.shape
    heads = cols // HD
    half = frames * tile_w // 2
    half_all = dev_n * half
    tok = 2 * half
    span = ((rows_y - 1) * (tile_w + 2) + tile_w) * frames
    line = (tile_w + 2) * frames
    full = (rows_y + 2) * line
    in_hbm = pl.BlockSpec(memory_space=pltpu.HBM)
    vmem = pl.BlockSpec(memory_space=pltpu.VMEM)
    dma = pltpu.SemaphoreType.DMA
    result = pl.pallas_call(
        functools.partial(kernel, dims),
        out_shape=jax.ShapeDtypeStruct((tok, dev_n * cols), BF16),
        in_specs=[in_hbm] * 7,
        out_specs=vmem,
        scratch_shapes=[
            pltpu.VMEM((frames, tile_w, rows_y, channels), BF16),
            pltpu.VMEM((rows_y, tile_w, frames, channels), F32),
            pltpu.VMEM(latent_weight.shape[::-1], BF16),
            pltpu.SMEM(lengths.shape, jnp.int32),
            pltpu.SMEM(clip_order.shape, jnp.int32),
            pltpu.VMEM((27, channels, channels), BF16),
            pltpu.VMEM((2 * HD, depth), BF16),
            pltpu.VMEM((3 * cols, depth), BF16),
            pltpu.VMEM((tile_w * frames, channels), BF16),
            pltpu.VMEM((tile_w * frames, channels), BF16),
            pltpu.VMEM((2, 2, frames, rows_y, channels), BF16),
            pltpu.VMEM((full, channels), F32),
            pltpu.VMEM((full, 3 * channels), BF16),
            pltpu.VMEM((2 * line + span, 3 * channels), BF16),
            pltpu.VMEM((span, channels), F32),
            pltpu.VMEM((half, LANES), BF16),
            pltpu.VMEM((grp_n, half, LANES), BF16),
            pltpu.VMEM((half, LANES), BF16),
            pltpu.VMEM((dev_n, half, LANES), BF16),
            pltpu.VMEM((half_all // 2, 2 * LANES), BF16),
            pltpu.VMEM((half_all // 2, 2 * LANES), BF16),
            pltpu.VMEM((2, 3 * cols, 2 * LANES), BF16),
            pltpu.VMEM((2, heads * LANES, 2 * LANES), BF16),
            pltpu.VMEM((2, heads * LANES, 2 * LANES), BF16),
            pltpu.VMEM((heads, half_all // LANES, LANES, 2 * LANES), BF16),
            pltpu.VMEM((heads, 2 * half_all, LANES), BF16),
            pltpu.VMEM((heads, LANES, 2 * half_all), BF16),
            pltpu.VMEM((heads, 2 * half_all, 2 * LANES), F32),
            pltpu.VMEM((3, half_all, LANES), BF16),
            pltpu.VMEM((dev_n, 3, half, LANES), BF16),
            dma((8,)),
            dma((5,)),
            dma((5,)),
            dma((grp_n,)),
            dma((grp_n,)),
            dma((dev_n,)),
            dma((dev_n,)),
            dma((dev_n,)),
            dma((dev_n,)),
        ],
        compiler_params=pltpu.CompilerParams(
            collective_id=0, has_side_effects=True, vmem_limit_bytes=42 * 1024 * 1024
        ),
    )(
        *(
            pltpu.with_memory_space_constraint(operand, pltpu.HBM)
            for operand in (
                features[0].transpose(0, 2, 1, 3),
                conv_weight.reshape(27, channels, channels),
                latent_weight.T,
                lengths,
                clip_order,
                embed_weight,
                qkv_weight.transpose(1, 2, 0).reshape(3 * cols, depth),
            )
        )
    )
    result = result.reshape(rows_y // 2, tile_w // 2, frames, dev_n * cols)
    return result.transpose(2, 0, 1, 3)[None]


def solution(mesh):
    dims = (mesh.shape["enc"], mesh.shape["grp"], mesh.shape["seq"])
    placed = (
        P("grp", None, "seq", "enc", None),
        P(),
        P(),
        P(),
        P(),
        P(),
        P(None, None, ("enc", "seq")),
    )
    return jax.shard_map(
        functools.partial(local, dims),
        mesh=mesh,
        in_specs=placed,
        out_specs=P("grp", None, "seq", "enc", None),
        check_vma=False,
    )
```

```python
import functools
import math

import jax
import jax.numpy as jnp
from jax import lax
from jax.experimental import pallas as pl
from jax.experimental.pallas import tpu as pltpu
from jax.sharding import PartitionSpec as P

HD = 64
LANES = 128
MESH = pl.DeviceIdType.MESH
F32 = jnp.float32
BF16 = jnp.bfloat16
NT = (((1,), (1,)), ((), ()))


def dot_nt(a, b):
    return lax.dot_general(a, b, NT, preferred_element_type=F32)


def lane_ids(rows):
    return lax.broadcasted_iota(jnp.int32, (rows, LANES), 1)


def silu(v):
    return (v / (1.0 + jnp.exp(-v))).astype(BF16)


def kernel(
    dims,
    feat_hbm,
    conv_hbm,
    lat_hbm,
    lengths_hbm,
    order_hbm,
    emb_hbm,
    qkv_hbm,
    out,
    raw,
    feat,
    lat_w,
    lengths,
    order,
    conv_w,
    emb,
    qkv,
    row_out,
    row_in,
    col_in,
    padded,
    even,
    odd,
    pre,
    patch,
    pool,
    chosen,
    gathered,
    tokens,
    key_tokens,
    wide,
    wqv,
    wk,
    queries,
    keys,
    values_t,
    scores,
    parcel,
    landed,
    load_sem,
    halo_send,
    halo_recv,
    pool_send,
    pool_recv,
    gather_send,
    gather_recv,
    parcel_send,
    parcel_recv,
):
    enc_n, grp_n, seq_n = dims
    dev_n = enc_n * seq_n
    enc, grp, seq = lax.axis_index("enc"), lax.axis_index("grp"), lax.axis_index("seq")
    me = enc * seq_n + seq
    other = 1 - seq
    rows_y, tile_w, frames, channels = feat.shape
    wide_x = tile_w + 2
    half = patch.shape[0]
    half_all = dev_n * half
    tok_all = 2 * half_all

    barrier = pltpu.get_barrier_semaphore()

    def greet_clip(step, carry):
        peer = lax.rem(me + step, dev_n)
        pl.semaphore_signal(
            barrier,
            inc=1,
            device_id={"enc": peer // seq_n, "seq": lax.rem(peer, seq_n)},
            device_id_type=MESH,
        )
        return carry

    def greet_pool(step, carry):
        pl.semaphore_signal(
            barrier,
            inc=1,
            device_id={"grp": lax.rem(grp + step, grp_n)},
            device_id_type=MESH,
        )
        return carry

    lax.fori_loop(1, dev_n, greet_clip, 0)
    lax.fori_loop(1, grp_n, greet_pool, 0)

    loads = []
    for slot, (src, dst) in enumerate(
        (
            (feat_hbm, raw),
            (conv_hbm, conv_w),
            (qkv_hbm, qkv),
            (emb_hbm, emb.at[pl.ds(0, HD)]),
            (emb_hbm, emb.at[pl.ds(HD, HD)]),
            (lat_hbm, lat_w),
            (lengths_hbm, lengths),
            (order_hbm, order),
        )
    ):
        copy = pltpu.make_async_copy(src, dst, load_sem.at[slot])
        copy.start()
        loads.append(copy)

    pl.semaphore_wait(barrier, dev_n - 1 + grp_n - 1)
    left, right = lax.rem(enc + enc_n - 1, enc_n), lax.rem(enc + 1, enc_n)
    columns = []
    for side, (target, x) in enumerate(((left, 0), (right, tile_w - 1))):
        for across in range(2):
            columns.append(
                pltpu.make_async_remote_copy(
                    src_ref=feat_hbm.at[:, x],
                    dst_ref=col_in.at[1 - side, across],
                    send_sem=halo_send.at[2 * side + across],
                    recv_sem=halo_recv.at[2 * side + across],
                    device_id={"enc": target, "seq": other if across else seq},
                    device_id_type=MESH,
                )
            )
    for copy in columns:
        copy.start()

    loads[0].wait()
    cells = raw[...].astype(F32).reshape(frames, tile_w * rows_y, channels)
    cells = jnp.swapaxes(cells, 0, 1).reshape(tile_w, rows_y, frames, channels)
    for y in range(rows_y):
        feat[y] = cells[:, y]

    edge_y = jnp.where(seq == 0, rows_y - 1, 0)
    row_out[...] = silu(feat[edge_y].reshape(tile_w * frames, channels))
    row_copy = pltpu.make_async_remote_copy(
        src_ref=row_out,
        dst_ref=row_in,
        send_sem=halo_send.at[4],
        recv_sem=halo_recv.at[4],
        device_id={"seq": other},
        device_id_type=MESH,
    )
    row_copy.start()

    line = wide_x * frames

    def place(y, x, value):
        start = (y * wide_x + x) * frames
        padded[pl.ds(start, value.shape[0])] = value

    for y in range(rows_y):
        inner = silu(feat[y].reshape(tile_w * frames, channels)).astype(F32)
        place(y + 1, 1, inner)

    row_copy.wait()
    row = row_in[...].astype(F32)
    place(0, 1, jnp.where(seq == 1, row, 0.0))
    place(rows_y + 1, 1, jnp.where(seq == 0, row, 0.0))
    for y in range(rows_y + 2):
        for x in (0, wide_x - 1):
            place(y, x, jnp.zeros((frames, channels), F32))

    def three_frames(cells):
        cells = cells.reshape(cells.shape[0] // frames, frames, channels)
        frame = lax.broadcasted_iota(jnp.int32, cells.shape, 1)
        for shift in range(3):
            back = 2 - shift
            moved = cells if back == 0 else pltpu.roll(cells, back, 1)
            yield shift, jnp.where(frame >= back, moved, 0.0).reshape(-1, channels)

    for dst, offset in ((even, 0), (odd, frames)):
        for shift, moved in three_frames(padded[pl.ds(offset, dst.shape[0])]):
            dst[:, pl.ds(shift * channels, channels)] = moved.astype(BF16)

    loads[1].wait()
    span = ((rows_y - 1) * wide_x + tile_w) * frames

    def taps(dy, carry):
        total = None
        for dx in range(3):
            src = odd if dx == 1 else even
            start = pl.multiple_of((dy * wide_x + (dx if dx == 2 else 0)) * frames, 2 * frames)
            for dt in range(3):
                term = jnp.dot(
                    src[pl.ds(start, span), pl.ds(dt * channels, channels)],
                    conv_w[(dt * 3 + dy) * 3 + dx],
                    preferred_element_type=F32,
                )
                total = term if total is None else total + term
        pre[...] = pre[...] + total
        return carry

    pre[...] = jnp.zeros_like(pre)
    lax.fori_loop(0, 3, taps, 0)

    for copy in columns:
        copy.wait()
    def correct(side, carry):
        present = jnp.where(side == 0, enc > 0, enc < enc_n - 1)
        beside, corner = (
            jnp.swapaxes(silu(col_in[side, across].astype(F32)).astype(F32), 0, 1)
            for across in range(2)
        )
        above = jnp.where(seq == 1, corner[rows_y - 1], 0.0)
        below = jnp.where(seq == 0, corner[0], 0.0)
        column = jnp.concatenate(
            [above, beside.reshape(rows_y * frames, channels), below], axis=0
        )
        column = jnp.where(present, column, 0.0)
        total = None
        for dt, moved in three_frames(column):
            for dy in range(3):
                term = jnp.dot(
                    moved[dy * frames : (dy + rows_y) * frames].astype(BF16),
                    conv_w[(dt * 3 + dy) * 3 + 2 * side],
                    preferred_element_type=F32,
                )
                total = term if total is None else total + term
        x = side * (tile_w - 1)
        for y in range(rows_y):
            rows = pl.ds(pl.multiple_of((y * wide_x + x) * frames, frames), frames)
            pre[rows] = pre[rows] + total[y * frames : (y + 1) * frames]
        return carry

    lax.fori_loop(0, 2, correct, 0)

    for copy in loads[5:]:
        copy.wait()
    lat_ch = lat_w.shape[0]
    own_len = lengths[grp]
    packed = None
    for y in range(rows_y):
        body = pre[pl.ds(y * line, tile_w * frames)] + feat[y].reshape(
            tile_w * frames, channels
        )
        body = body.reshape(tile_w // 2, 2, frames, channels)
        for b in range(2):
            hidden = body[:, b].reshape(half, channels).astype(BF16)
            first = (y * 2 + b) * lat_ch
            parts = []
            if first:
                parts.append(jnp.zeros((first, channels), BF16))
            parts.append(lat_w[...])
            if first + lat_ch < LANES:
                parts.append(jnp.zeros((LANES - first - lat_ch, channels), BF16))
            term = dot_nt(hidden, jnp.concatenate(parts, axis=0))
            packed = term if packed is None else packed + term
    frame = lax.rem(lax.broadcasted_iota(jnp.int32, (half, LANES), 0), frames)
    patch[...] = jnp.where(frame < own_len, packed, 0.0).astype(BF16)

    source = jnp.int32(0)
    for n in range(grp_n):
        source = source + jnp.where(order[n] == grp, n, 0)
    source = jnp.minimum(source, grp_n - 1)
    clip_len = lengths[source]

    def pool_copy(peer, slot):
        return pltpu.make_async_remote_copy(
            src_ref=patch,
            dst_ref=pool.at[slot],
            send_sem=pool_send.at[peer],
            recv_sem=pool_recv.at[slot],
            device_id={"grp": peer},
            device_id_type=MESH,
        )

    def pool_start(step, carry):
        pool_copy(lax.rem(grp + step, grp_n), grp).start()
        return carry

    def pool_wait(step, carry):
        peer = lax.rem(grp + step, grp_n)
        pool_copy(peer, peer).wait()
        return carry

    lax.fori_loop(1, grp_n, pool_start, 0)
    pool[grp] = patch[...]

    for copy in loads[2:5]:
        copy.wait()
    folded = dot_nt(qkv[...], emb[...])
    high = folded.astype(BF16).astype(F32)
    low = folded - high
    lane = lane_ids(folded.shape[0])
    for part in range(2):
        keep = (lane >= HD) if part else (lane < HD)
        wide[part, :, pl.ds(0, LANES)] = jnp.where(keep, high, 0.0).astype(BF16)
        wide[part, :, pl.ds(LANES, LANES)] = jnp.where(keep, low, 0.0).astype(BF16)
    heads = qkv.shape[0] // 3 // HD
    for part in range(2):
        for place_h in range(heads):
            source_h = lax.rem(place_h + seq, heads)

            def block(which):
                start = pl.multiple_of((which * heads + source_h) * HD, HD)
                return wide[part, pl.ds(start, HD)]

            first = place_h * LANES
            wqv[part, pl.ds(first, HD)] = block(0)
            wqv[part, pl.ds(first + HD, HD)] = block(2)
            wk[part, pl.ds(place_h * LANES, HD)] = block(1)
            wk[part, pl.ds(place_h * LANES + HD, HD)] = block(1)

    row = lax.broadcasted_iota(jnp.int32, (HD, tok_all), 0)
    frame = lax.rem(lax.broadcasted_iota(jnp.int32, (HD, tok_all), 1), frames)
    counted = jnp.where((row == 0) & (frame < clip_len), 1.0, 0.0).astype(BF16)
    for head in range(heads):
        values_t[head, pl.ds(HD, HD)] = counted

    lax.fori_loop(1, grp_n, pool_wait, 0)
    chosen[...] = pool[source]

    def owner_at(slot):
        return lax.rem(enc + 1 + slot // 2, enc_n), lax.rem(seq + 1 + slot, 2)

    def mirror(slot):
        return 2 * lax.rem(2 * enc_n - 2 - slot // 2, enc_n) + lax.rem(slot, 2)

    def gather_copy(slot):
        owner_enc, owner_seq = owner_at(slot)
        return pltpu.make_async_remote_copy(
            src_ref=chosen,
            dst_ref=gathered.at[mirror(slot)],
            send_sem=gather_send.at[slot],
            recv_sem=gather_recv.at[mirror(slot)],
            device_id={"enc": owner_enc, "seq": owner_seq},
            device_id_type=MESH,
        )

    def gather_start(slot, carry):
        gather_copy(slot).start()
        return carry

    def gather_arrived(slot, carry):
        pltpu.make_async_remote_copy(
            src_ref=chosen,
            dst_ref=gathered.at[slot],
            send_sem=gather_send.at[slot],
            recv_sem=gather_recv.at[slot],
            device_id={"enc": owner_at(slot)[0], "seq": owner_at(slot)[1]},
            device_id_type=MESH,
        ).wait()
        return carry

    group_n = dev_n // 2
    lax.fori_loop(group_n - 2, dev_n - 2, gather_start, 0)
    lax.fori_loop(0, group_n - 2, gather_start, 0)
    gather_start(dev_n - 2, 0)
    gathered[dev_n - 1] = chosen[...]

    factor = HD**-0.5 * math.log2(math.e)
    group = group_n * half
    blocks_group = group // LANES

    def project(at, carry):
        lax.fori_loop(
            at * group_n, jnp.minimum((at + 1) * group_n, dev_n - 1), gather_arrived, 0
        )
        cells = gathered[pl.ds(at * group_n, group_n)].reshape(group, LANES)
        tokens[:, pl.ds(0, LANES)] = cells
        tokens[:, pl.ds(LANES, LANES)] = cells
        wide_cells = cells.astype(F32).reshape(group // frames, frames, LANES)
        frame = lax.broadcasted_iota(jnp.int32, wide_cells.shape, 1)
        kept = jnp.where(frame < clip_len, wide_cells, wide_cells[:, :1])
        kept = kept.reshape(group, LANES).astype(BF16)
        key_tokens[:, pl.ds(0, LANES)] = kept
        key_tokens[:, pl.ds(LANES, LANES)] = kept
        for part in range(2):
            first = pl.multiple_of(part * half_all + at * group, LANES)
            made = dot_nt(key_tokens[...], wk[part])
            for head in range(heads):
                keys[head, pl.ds(first, group)] = made[:, head * LANES : (head + 1) * LANES].astype(
                    BF16
                )
            made = dot_nt(wqv[part], tokens[...])
            for head in range(heads):
                query = made[head * LANES : head * LANES + HD]
                query = query.astype(BF16).astype(F32) * factor
                high = query.astype(BF16)
                low = (query - high.astype(F32)).astype(BF16)
                for block in range(blocks_group):
                    cut = slice(block * LANES, (block + 1) * LANES)
                    spot = queries.at[head, at * blocks_group + block, :, pl.ds(part * LANES, LANES)]
                    spot[pl.ds(0, HD)] = high[:, cut]
                    spot[pl.ds(HD, HD)] = low[:, cut]
                values_t[head, pl.ds(0, HD), pl.ds(first, group)] = made[
                    head * LANES + HD : (head + 1) * LANES
                ].astype(BF16)
        return carry

    lax.fori_loop(0, 2, project, 0)

    chunk = tok_all // 2
    width = 2 * LANES
    block_n = half_all // LANES

    def score(head, block, start, peak):
        cut = pl.ds(start, chunk)
        made = jnp.dot(keys[head, cut], queries[head, block], preferred_element_type=F32)
        scores[head, cut] = made
        made = jnp.max(made.reshape(chunk // 8, 8, width), axis=0)
        return made if peak is None else jnp.maximum(peak, made)

    frame = lax.rem(lax.broadcasted_iota(jnp.int32, (HD, width), 1), frames)
    alive = frame < clip_len

    def parcel_copy(slot):
        owner_enc, owner_seq = owner_at(slot)
        return pltpu.make_async_remote_copy(
            src_ref=parcel.at[:, pl.ds(pl.multiple_of(slot * half, half), half)],
            dst_ref=landed.at[me],
            send_sem=parcel_send.at[slot],
            recv_sem=parcel_recv.at[me],
            device_id={"enc": owner_enc, "seq": owner_seq},
            device_id_type=MESH,
        )

    def parcel_start(slot, carry):
        parcel_copy(slot).start()
        return carry

    def parcel_wait(slot, carry):
        owner_enc, owner_seq = owner_at(slot)
        owner = owner_enc * seq_n + owner_seq
        pltpu.make_async_remote_copy(
            src_ref=parcel.at[:, pl.ds(pl.multiple_of(slot * half, half), half)],
            dst_ref=landed.at[owner],
            send_sem=parcel_send.at[slot],
            recv_sem=parcel_recv.at[owner],
            device_id={"enc": owner_enc, "seq": owner_seq},
            device_id_type=MESH,
        ).wait()
        return carry

    def attend(block, peak):
        outputs = []
        for head in range(heads):
            top = jnp.max(peak, axis=0, keepdims=True)
            peak, summed = None, None
            if head + 1 < heads:
                next_head, next_block = head + 1, block
            else:
                next_head, next_block = 0, lax.rem(block + 1, block_n)
            for start in range(0, tok_all, chunk):
                peak = score(next_head, next_block, start, peak)
                cut = pl.ds(start, chunk)
                weight = jnp.exp2(scores[head, cut] - top).astype(BF16)
                term = jnp.dot(values_t[head, :, cut], weight, preferred_element_type=F32)
                summed = term if summed is None else summed + term
            outputs.append(jnp.where(alive, summed[:HD] / summed[HD : HD + 1], 0.0))
        rows = pl.ds(pl.multiple_of(block * LANES, LANES), LANES)
        pair = jnp.concatenate(outputs[:2], axis=0).T.astype(BF16)
        parcel[0, rows] = pair[:LANES]
        parcel[1, rows] = pair[LANES:]
        first, second = outputs[2][:, :LANES], outputs[2][:, LANES:]
        mixed = jnp.concatenate(
            [jnp.where(seq == 0, first, second), jnp.where(seq == 0, second, first)], axis=0
        )
        parcel[2, rows] = mixed.T.astype(BF16)
        lax.fori_loop(
            block * LANES // half,
            jnp.minimum((block + 1) * LANES // half, dev_n - 1),
            parcel_start,
            0,
        )
        return peak

    peak = None
    for start in range(0, tok_all, chunk):
        peak = score(0, 0, start, peak)
    lax.fori_loop(0, block_n, attend, peak)
    landed[me] = parcel[:, pl.ds((dev_n - 1) * half, half)]
    lax.fori_loop(0, dev_n - 1, parcel_wait, 0)

    low = lane_ids(half) < HD
    for couple in range(enc_n):
        first, second = seq_n * couple, seq_n * couple + 1
        base = couple * 3 * LANES
        for part in range(2):
            rows = pl.ds(part * half, half)
            out[rows, pl.ds(base, LANES)] = landed[first, part]
            out[rows, pl.ds(base + 2 * LANES, LANES)] = landed[second, part]
        ahead = landed[first, 2].astype(F32)
        behind = landed[second, 2].astype(F32)
        out[pl.ds(0, half), pl.ds(base + LANES, LANES)] = jnp.where(low, ahead, behind).astype(BF16)
        out[pl.ds(half, half), pl.ds(base + LANES, LANES)] = pltpu.roll(
            jnp.where(low, behind, ahead), HD, 1
        ).astype(BF16)


def local(dims, features, conv_weight, latent_weight, lengths, clip_order, embed_weight, qkv_weight):
    enc_n, grp_n, seq_n = dims
    dev_n = enc_n * seq_n
    _, frames, rows_y, tile_w, channels = features.shape
    depth, _, cols = qkv_weight.shape
    heads = cols // HD
    half = frames * tile_w // 2
    half_all = dev_n * half
    tok = 2 * half
    span = ((rows_y - 1) * (tile_w + 2) + tile_w) * frames
    line = (tile_w + 2) * frames
    full = (rows_y + 2) * line
    in_hbm = pl.BlockSpec(memory_space=pltpu.HBM)
    vmem = pl.BlockSpec(memory_space=pltpu.VMEM)
    dma = pltpu.SemaphoreType.DMA
    result = pl.pallas_call(
        functools.partial(kernel, dims),
        out_shape=jax.ShapeDtypeStruct((tok, dev_n * cols), BF16),
        in_specs=[in_hbm] * 7,
        out_specs=vmem,
        scratch_shapes=[
            pltpu.VMEM((frames, tile_w, rows_y, channels), BF16),
            pltpu.VMEM((rows_y, tile_w, frames, channels), F32),
            pltpu.VMEM(latent_weight.shape[::-1], BF16),
            pltpu.SMEM(lengths.shape, jnp.int32),
            pltpu.SMEM(clip_order.shape, jnp.int32),
            pltpu.VMEM((27, channels, channels), BF16),
            pltpu.VMEM((2 * HD, depth), BF16),
            pltpu.VMEM((3 * cols, depth), BF16),
            pltpu.VMEM((tile_w * frames, channels), BF16),
            pltpu.VMEM((tile_w * frames, channels), BF16),
            pltpu.VMEM((2, 2, frames, rows_y, channels), BF16),
            pltpu.VMEM((full, channels), F32),
            pltpu.VMEM((full, 3 * channels), BF16),
            pltpu.VMEM((2 * line + span, 3 * channels), BF16),
            pltpu.VMEM((span, channels), F32),
            pltpu.VMEM((half, LANES), BF16),
            pltpu.VMEM((grp_n, half, LANES), BF16),
            pltpu.VMEM((half, LANES), BF16),
            pltpu.VMEM((dev_n, half, LANES), BF16),
            pltpu.VMEM((half_all // 2, 2 * LANES), BF16),
            pltpu.VMEM((half_all // 2, 2 * LANES), BF16),
            pltpu.VMEM((2, 3 * cols, 2 * LANES), BF16),
            pltpu.VMEM((2, heads * LANES, 2 * LANES), BF16),
            pltpu.VMEM((2, heads * LANES, 2 * LANES), BF16),
            pltpu.VMEM((heads, half_all // LANES, LANES, 2 * LANES), BF16),
            pltpu.VMEM((heads, 2 * half_all, LANES), BF16),
            pltpu.VMEM((heads, LANES, 2 * half_all), BF16),
            pltpu.VMEM((heads, 2 * half_all, 2 * LANES), F32),
            pltpu.VMEM((3, half_all, LANES), BF16),
            pltpu.VMEM((dev_n, 3, half, LANES), BF16),
            dma((8,)),
            dma((5,)),
            dma((5,)),
            dma((grp_n,)),
            dma((grp_n,)),
            dma((dev_n,)),
            dma((dev_n,)),
            dma((dev_n,)),
            dma((dev_n,)),
        ],
        compiler_params=pltpu.CompilerParams(
            collective_id=0, has_side_effects=True, vmem_limit_bytes=42 * 1024 * 1024
        ),
    )(
        *(
            pltpu.with_memory_space_constraint(operand, pltpu.HBM)
            for operand in (
                features[0].transpose(0, 2, 1, 3),
                conv_weight.reshape(27, channels, channels),
                latent_weight.T,
                lengths,
                clip_order,
                embed_weight,
                qkv_weight.transpose(1, 2, 0).reshape(3 * cols, depth),
            )
        )
    )
    result = result.reshape(rows_y // 2, tile_w // 2, frames, dev_n * cols)
    return result.transpose(2, 0, 1, 3)[None]


def solution(mesh):
    dims = (mesh.shape["enc"], mesh.shape["grp"], mesh.shape["seq"])
    placed = (
        P("grp", None, "seq", "enc", None),
        P(),
        P(),
        P(),
        P(),
        P(),
        P(None, None, ("enc", "seq")),
    )
    return jax.shard_map(
        functools.partial(local, dims),
        mesh=mesh,
        in_specs=placed,
        out_specs=P("grp", None, "seq", "enc", None),
        check_vma=False,
    )
```
